512 devices in a mesh: dp: 16 (over z_lo, core), context: 8 (over z_hi, y), tensor: 4 (over x).
Axes of the slice: x: 4, y: 4, z: 16 (z_hi: 2, z_lo: 8; z = z_hi * 8 + z_lo), core: 2. Of those that a mesh axis runs over, the one named last changes fastest.
Arguments:
- latent: bfloat16 [16, 1024, 512], P('dp', 'context'), may hold values from -6 to 6
- key_rope: bfloat16 [16, 1024, 1024], P('dp', 'context', 'tensor'), may hold values from -6 to 6
- query: bfloat16 [16, 1024, 4096], P('dp', 'context', 'tensor'), may hold values from -600 to 600
- out_grad: bfloat16 [16, 1024, 4096], P('dp', 'context', 'tensor'), may hold values from -6 to 6
- positions: int32 [16, 1024], P('dp', 'context'), may hold values from 0 to 1023, as said below
- freq_index: int32 [32, 16], P('tensor'), may hold values from 0 to 63, all different within a row
- up_key: bfloat16 [512, 3072], P(('dp', 'context'), 'tensor'), may hold values from -0.25 to 0.25
- up_value: bfloat16 [512, 4096], P(('dp', 'context'), 'tensor'), may hold values from -0.25 to 0.25
Outputs:
- query_grad: bfloat16 [16, 1024, 4096], P('dp', 'context', 'tensor')
- key_rope_grad: bfloat16 [16, 1024, 1024], P('dp', 'context', 'tensor')
- latent_grad: bfloat16 [16, 1024, 512], P('dp', 'context')
- up_key_grad: bfloat16 [512, 3072], P(('dp', 'context'), 'tensor')
- up_value_grad: bfloat16 [512, 4096], P(('dp', 'context'), 'tensor')
The draws below stay inside these ranges and needn't reach their ends.
Inputs may be any that keep to these rules, and one draw needn't show every extreme that they name: In each sequence every position 0 to 1023 appears once, in 16 runs of 64 consecutive increasing positions that start at multiples of 64; each device along context holds two runs, in any order. `freq_index`: each row names 16 different frequency pairs.
All inputs are finite; a program needn't handle non-finite values.
Results may differ from the reference program's by a relative error of at most 0.018.
Values may be sent and summed in bfloat16 or wider, within the bound.
No kernel may reach another device: no remote copies, remote signals or barrier semaphores. Data moves between devices by JAX's collectives and lax.ppermute only.
A program may use at most 64 MiB of HBM per device.

```python
import jax
import jax.numpy as jnp
from jax import lax

R = 512
HEADS = 32
HD = 128
VD = 128
RK = 16
FREQS = 64
NOPE = 96
SEQ = 1024
BATCH = 16
HALF = 64
RUNS = 16


def shared_rope(key):
    return jnp.clip(jax.random.normal(key, (BATCH, SEQ, HEADS * 2 * RK), jnp.float32), -6.0, 6.0)


def draw_key_rope(key, part):
    shared = shared_rope(key)
    return shared.astype(jnp.bfloat16)


def draw_query(key, part):
    key = jax.random.fold_in(key, 7)
    baseline = jnp.clip(jax.random.normal(key, (BATCH, SEQ, HEADS, HD), jnp.float32), -6.0, 6.0)
    return baseline.reshape(BATCH, SEQ, HEADS * HD).astype(jnp.bfloat16)


def draw_positions(key, part):
    key = jax.random.fold_in(key, 11)
    row_keys = jax.random.split(key, BATCH)

    def one_row(row_key):
        ordering = jax.random.permutation(row_key, RUNS)
        starts = ordering * HALF
        return (starts[:, None] + jnp.arange(HALF)[None, :]).reshape(RUNS * HALF)
    return jax.vmap(one_row)(row_keys).astype(jnp.int32)


def steps_of(key, shape, cuts, low, high):
    gain = 1.0
    for position, shards_of in cuts:
        draws = jax.random.uniform(jax.random.fold_in(jax.random.fold_in(key, 6), position), (shards_of,), jnp.float32, low / len(cuts), high / len(cuts))
        gain = gain * jnp.repeat(jnp.exp(draws), shape[position] // shards_of).reshape((-1,) + (1,) * (len(shape) - 1 - position))
    return gain


def different_ones(rng, rows, number_of, top, lift):
    sequence = jax.random.permutation(jax.random.fold_in(rng, 1), number_of)
    favour = sequence
    for power in range(3):
        favour = favour * favour // number_of
    favour = favour * lift // number_of
    chance = jax.random.randint(jax.random.fold_in(rng, 2), (rows, number_of), 0, 4096) + favour
    fixed_rows = jax.random.permutation(jax.random.fold_in(rng, 3), rows)[jnp.arange(number_of) % rows]
    chance = jnp.where(jnp.arange(rows)[:, None] == fixed_rows[None, :], 1 << 14, chance)
    merit = chance * number_of + jnp.arange(number_of)
    return lax.top_k(merit.astype(jnp.int32), top)[1].astype(jnp.int32)


def scatter_about(rng, dims, scale, limit, cuts=(), kind=jnp.bfloat16):
    entries = scale * jax.random.normal(rng, dims, jnp.float32)
    if cuts:
        entries = entries * steps_of(rng, dims, cuts, -0.22, 0.18)
    return jnp.clip(entries, -limit, limit).astype(kind)


def setup_inputs(seed: int = 0) -> dict:
    keys = jax.random.split(jax.random.key(seed), 9)
    return {
        "latent": scatter_about(keys[0], (BATCH, SEQ, R), 1.0, 6.0, ((0, 16), (1, 8))),
        "key_rope": draw_key_rope(jax.random.fold_in(keys[8], 71), 0),
        "query": draw_query(jax.random.fold_in(keys[8], 71), 0),
        "out_grad": scatter_about(keys[3], (BATCH, SEQ, HEADS * VD), 1.0, 6.0, ((0, 16), (1, 8), (2, 4))),
        "positions": draw_positions(jax.random.fold_in(keys[8], 71), 0),
        "freq_index": different_ones(keys[5], HEADS, FREQS, RK, 0),
        "up_key": scatter_about(keys[6], (R, HEADS * NOPE), R ** -0.5, 0.25, ((0, 128), (1, 4))),
        "up_value": scatter_about(keys[7], (R, HEADS * VD), R ** -0.5, 0.25, ((0, 128), (1, 4))),
    }


rope_base = 500000.0
neg_large = -1.0e30


def rope_tables(places, freq_index, head_dim):
    inverse = rope_base ** (-2.0 * freq_index.astype(jnp.float32) / head_dim)
    angles = places.astype(jnp.float32)[:, None, None] * inverse[None]
    return jnp.cos(angles), jnp.sin(angles)


def rotate(values, cosine, sine_table):
    width = cosine.shape[-1]
    first = values[..., :width]
    second = values[..., width:]
    return jnp.concatenate([first * cosine - second * sine_table, second * cosine + first * sine_table], -1)


def unrotate(values, cosine, sine_table):
    width = cosine.shape[-1]
    first = values[..., :width]
    second = values[..., width:]
    return jnp.concatenate([first * cosine + second * sine_table, second * cosine - first * sine_table], -1)


def to_float(array):
    return array.astype(jnp.float32)


def one_sequence(freq_index, up_key, up_value, inputs):
    latent, key_rope, query, out_grad, places = inputs
    length = latent.shape[0]
    score_scale = HD ** -0.5
    rope_dims = 2 * RK
    cosine, sine_table = rope_tables(places, freq_index, HD)
    key_nope = jnp.dot(latent, up_key, preferred_element_type=jnp.float32).astype(jnp.bfloat16).reshape(length, HEADS, NOPE)
    values = jnp.dot(latent, up_value, preferred_element_type=jnp.float32).astype(jnp.bfloat16).reshape(length, HEADS, VD)
    key_rot = rotate(to_float(key_rope.reshape(length, HEADS, rope_dims)), cosine, sine_table).astype(jnp.bfloat16)
    query_heads = query.reshape(length, HEADS, HD)
    query_rot = rotate(to_float(query_heads[..., :rope_dims]), cosine, sine_table).astype(jnp.bfloat16)
    query_nope = query_heads[..., rope_dims:]
    grad_out = out_grad.reshape(length, HEADS, VD)
    scores = score_scale * (jnp.einsum('ihd,jhd->hij', to_float(query_rot), to_float(key_rot))
                            + jnp.einsum('ihd,jhd->hij', to_float(query_nope), to_float(key_nope)))
    visible = places[None, :] <= places[:, None]
    masked = jnp.where(visible[None], scores, -jnp.inf)
    running_max = jnp.max(masked, -1, keepdims=True)
    log_total = running_max[..., 0] + jnp.log(jnp.sum(jnp.exp(masked - running_max), -1))
    exact_probs = jnp.exp(jnp.where(visible[None], scores - log_total[..., None], neg_large))
    attn = jnp.einsum('hij,jhv->ihv', exact_probs, to_float(values), precision=lax.Precision.HIGHEST)
    probs = exact_probs.astype(jnp.bfloat16)
    row_delta = jnp.sum(to_float(grad_out) * attn, -1)
    dprob = jnp.einsum('ihv,jhv->hij', to_float(grad_out), to_float(values))
    score_grad = (score_scale * to_float(probs) * (dprob - row_delta.T[:, :, None])).astype(jnp.bfloat16)
    grad_qrot = jnp.einsum('hij,jhd->ihd', to_float(score_grad), to_float(key_rot))
    grad_qnope = jnp.einsum('hij,jhd->ihd', to_float(score_grad), to_float(key_nope))
    query_grad = jnp.concatenate([unrotate(grad_qrot, cosine, sine_table), grad_qnope], -1)
    query_grad = query_grad.astype(jnp.bfloat16).reshape(length, HEADS * HD)
    grad_krot = jnp.einsum('hij,ihd->jhd', to_float(score_grad), to_float(query_rot))
    key_rope_grad = unrotate(grad_krot, cosine, sine_table).astype(jnp.bfloat16).reshape(length, HEADS * rope_dims)
    key_nope_grad = jnp.einsum('hij,ihd->jhd', to_float(score_grad), to_float(query_nope)).astype(jnp.bfloat16)
    values_grad = jnp.einsum('hij,ihv->jhv', to_float(probs), to_float(grad_out)).astype(jnp.bfloat16)
    key_nope_grad = key_nope_grad.reshape(length, HEADS * NOPE)
    values_grad = values_grad.reshape(length, HEADS * VD)
    latent_grad = (jnp.dot(key_nope_grad, up_key.T, preferred_element_type=jnp.float32)
                   + jnp.dot(values_grad, up_value.T, preferred_element_type=jnp.float32)).astype(jnp.bfloat16)
    key_term = jnp.dot(latent.T, key_nope_grad, preferred_element_type=jnp.float32)
    value_term = jnp.dot(latent.T, values_grad, preferred_element_type=jnp.float32)
    return query_grad, key_rope_grad, latent_grad, key_term, value_term


def reference(latent, key_rope, query, out_grad, positions, freq_index, up_key, up_value):
    results = lax.map(partial_sequence(freq_index, up_key, up_value), (latent, key_rope, query, out_grad, positions))
    query_grad, key_rope_grad, latent_grad, key_terms, value_terms = results
    up_key_grad = jnp.sum(key_terms, 0).astype(jnp.bfloat16)
    up_value_grad = jnp.sum(value_terms, 0).astype(jnp.bfloat16)
    return (query_grad, key_rope_grad, latent_grad, up_key_grad, up_value_grad)


def partial_sequence(freq_index, up_key, up_value):
    def apply_one(inputs):
        return one_sequence(freq_index, up_key, up_value, inputs)
    return apply_one
```

```python
import jax
import jax.numpy as jnp
from jax import lax
from jax.experimental import pallas as pl
from jax.experimental.pallas import tpu as pltpu
from jax.sharding import Mesh, PartitionSpec as P

rope_base = 500000.0
neg_large = -1e30
log2_e = 1.4426950408889634

CTX = 8
TOK = 128
SEQ = CTX * TOK
HD = 128
RD = 32
HALF_RD = 16
NOPE = 96
RANK = 512
ROWS = 4
ZL = 8
CORE = 2
TEN = 4
Q0, G0, K0, W0, MSG = 0, 128, 256, 288, 304
BLK = 256

f32 = jnp.float32
bf16 = jnp.bfloat16


def dot(a, b, dims=((1,), (0,))):
    return lax.dot_general(a, b, (dims, ((), ())), preferred_element_type=f32)


def pack_kernel(q_ref, g_ref, kr_ref, wk_ref, wv_ref, pos_ref, out_ref):
    rope_t = kr_ref[...].astype(f32).T.astype(bf16)
    pos = pos_ref[...]
    high = (pos >> 6).astype(f32)
    low = (pos & 63).astype(f32)
    wk = wk_ref[...].astype(f32)
    wv = wv_ref[...].astype(f32)
    for h in range(CTX):
        out_ref[h, Q0:Q0 + TOK, :] = q_ref[:, h * HD:(h + 1) * HD]
        out_ref[h, G0:G0 + TOK, :] = g_ref[:, h * HD:(h + 1) * HD]
        out_ref[h, K0:K0 + RD, :] = rope_t[h * RD:(h + 1) * RD, :]
        wk_h = jnp.concatenate([jnp.zeros((ROWS, RD), f32), wk[:, h * NOPE:(h + 1) * NOPE]], 1)
        tail = jnp.concatenate(
            [wv[:, h * HD:(h + 1) * HD], wk_h, high, low, jnp.zeros((6, TOK), f32)], 0
        )
        out_ref[h, W0:MSG, :] = tail.astype(bf16)


def pack(query, out_grad, key_rope, up_key, up_value, positions):
    return pl.pallas_call(
        pack_kernel,
        out_shape=jax.ShapeDtypeStruct((CTX, MSG, HD), bf16),
        name="pack",
    )(query, out_grad, key_rope, up_key, up_value, positions)


def main_kernel(
    zh_ref, inv_ref, msg_ref, lat_ref, w_ref,
    dq_ref, dkr_ref, dlat_ref, dw_ref,
    lat_s, w_s, k_s, kt_s, q_s, qt_s, v_s, gt_s, pos_s, cos_s, sin_s, dkv_s, dqt_s,
):
    zh = zh_ref[0]
    for z in range(2):
        for y in range(4):
            c = z * 4 + y
            lat_s[c * TOK:(c + 1) * TOK, :] = lat_ref[y, z ^ zh]
    for z in range(ZL):
        for c in range(CORE):
            r = (z * CORE + c) * 32
            w_s[r:r + 32, HD:2 * HD] = w_ref[c, z, 0:32, :]
            w_s[r:r + 32, 0:HD] = w_ref[c, z, 32:64, :]
    for c in range(CTX):
        tail = msg_ref[c, W0:MSG, :].astype(f32)
        pos_s[0:1, c * TOK:(c + 1) * TOK] = tail[8:9] * 64.0 + tail[9:10]
    pos_row = pos_s[0:1, :]
    angles = inv_ref[...] * pos_row
    cos_s[...] = jnp.cos(angles)
    sin_s[...] = jnp.sin(angles)
    cos = cos_s[...]
    sin = sin_s[...]

    def rot(x):
        a, b = x[:HALF_RD], x[HALF_RD:RD]
        return jnp.concatenate([a * cos - b * sin, b * cos + a * sin], 0)

    kr = jnp.concatenate([msg_ref[c, K0:K0 + RD, :] for c in range(CTX)], 1).astype(f32)
    kr_pad = jnp.concatenate([rot(kr), jnp.zeros((HD - RD, SEQ), f32)], 0)
    kv = dot(lat_s[...], w_s[...])
    k = (kv[:, :HD] + kr_pad.T).astype(bf16)
    k_s[...] = k
    kt_s[...] = k.astype(f32).T.astype(bf16)
    v_s[...] = kv[:, HD:].astype(bf16)
    for c in range(CTX):
        qt_s[:, c * TOK:(c + 1) * TOK] = msg_ref[c, Q0:Q0 + TOK, :].astype(f32).T
        gt_s[:, c * TOK:(c + 1) * TOK] = msg_ref[c, G0:G0 + TOK, :].astype(f32).T.astype(bf16)
    qt_s[0:RD, :] = rot(qt_s[0:RD, :])
    qt = qt_s[...]
    q_s[...] = qt.T.astype(bf16)
    pos_col = jnp.broadcast_to(pos_row, (8, SEQ)).T[:, 0:1]
    scale = HD ** -0.5
    dkv_s[...] = jnp.zeros_like(dkv_s)

    for b in range(SEQ // BLK):
        cols = slice(b * BLK, (b + 1) * BLK)
        st = dot(k_s[...], qt[:, cols].astype(bf16))
        visible = pos_col <= pos_row[:, cols]
        st = jnp.where(visible, st * (scale * log2_e), neg_large)
        top = jnp.max(st, 0, keepdims=True)
        e = jnp.exp2(st - top)
        dp = dot(v_s[...], gt_s[:, cols])
        total = jnp.sum(e, 0, keepdims=True)
        weighted = jnp.sum(e * dp, 0, keepdims=True)
        inv_total = 1.0 / total
        delta = weighted * inv_total
        probs = (e * inv_total).astype(bf16)
        ds = (scale * probs.astype(f32) * (dp - delta)).astype(bf16)
        dqt_s[:, cols] = dot(kt_s[...], ds)
        dkv_s[:, 0:HD] += dot(ds, q_s[cols, :])
        grad = jnp.concatenate(
            [msg_ref[c, G0:G0 + TOK, :] for c in range(b * BLK // TOK, (b + 1) * BLK // TOK)], 0
        )
        dkv_s[:, HD:] += dot(probs, grad)

    def unrot(x):
        a, b = x[:HALF_RD], x[HALF_RD:RD]
        return jnp.concatenate([a * cos + b * sin, b * cos - a * sin], 0)

    dqt_s[0:RD, :] = unrot(dqt_s[0:RD, :])
    dq = dqt_s[...].T.astype(bf16)
    dkr = unrot(dkv_s[:, 0:HD].T[0:RD, :]).astype(bf16)
    for c in range(CTX):
        dq_ref[c] = dq[c * TOK:(c + 1) * TOK, :]
        dkr_ref[c] = dkr[:, c * TOK:(c + 1) * TOK]
    dkv = dkv_s[...].astype(bf16)
    dlat = dot(dkv, w_s[...], ((1,), (1,))).astype(bf16)
    for t in range(TEN):
        dlat_ref[t] = dlat[:, t * HD:(t + 1) * HD]
    dw = dot(lat_s[...], dkv, ((0,), (0,))).astype(bf16)
    for z in range(ZL):
        for c in range(CORE):
            r = (z * CORE + c) * 32
            dw_ref[c, z] = dw[r:r + 32, :]


def attention(zh, inverse, msg, lat, w):
    smem = pl.BlockSpec(memory_space=pltpu.SMEM)
    vmem = pl.BlockSpec(memory_space=pltpu.VMEM)
    return pl.pallas_call(
        main_kernel,
        in_specs=[smem, vmem, vmem, vmem, vmem],
        out_specs=[vmem] * 4,
        out_shape=[
            jax.ShapeDtypeStruct((CTX, TOK, HD), bf16),
            jax.ShapeDtypeStruct((CTX, RD, TOK), bf16),
            jax.ShapeDtypeStruct((TEN, SEQ, HD), bf16),
            jax.ShapeDtypeStruct((CORE, ZL, 32, 2 * HD), bf16),
        ],
        scratch_shapes=[
            pltpu.VMEM((SEQ, RANK), bf16),
            pltpu.VMEM((RANK, 2 * HD), bf16),
            pltpu.VMEM((SEQ, HD), bf16),
            pltpu.VMEM((HD, SEQ), bf16),
            pltpu.VMEM((SEQ, HD), bf16),
            pltpu.VMEM((HD, SEQ), f32),
            pltpu.VMEM((SEQ, HD), bf16),
            pltpu.VMEM((HD, SEQ), bf16),
            pltpu.VMEM((8, SEQ), f32),
            pltpu.VMEM((HALF_RD, SEQ), f32),
            pltpu.VMEM((HALF_RD, SEQ), f32),
            pltpu.VMEM((SEQ, 2 * HD), f32),
            pltpu.VMEM((HD, SEQ), f32),
        ],
        compiler_params=pltpu.CompilerParams(vmem_limit_bytes=56 * 1024 * 1024),
        name="attention_backward",
    )(zh, inverse, msg, lat, w)


def combine_kernel(dq_ref, dkr_ref, lat_ref, dw_ref, out_ref):
    dw = jnp.sum(dw_ref[...].astype(f32), 0)
    for c in range(CTX):
        out_ref[c, 0:TOK, :] = dq_ref[c]
        out_ref[c, K0:K0 + RD, :] = dkr_ref[c]
        rows = slice(c * TOK, (c + 1) * TOK)
        out_ref[c, G0:G0 + TOK, :] = jnp.sum(lat_ref[:, rows, :].astype(f32), 0).astype(bf16)
        part = dw[c * ROWS:(c + 1) * ROWS, :]
        tail = jnp.concatenate([part[:, HD:], part[:, :HD], jnp.zeros((8, HD), f32)], 0)
        out_ref[c, W0:MSG, :] = tail.astype(bf16)


def combine(dq, dkr, lat, dw):
    return pl.pallas_call(
        combine_kernel,
        out_shape=jax.ShapeDtypeStruct((CTX, MSG, HD), bf16),
        name="combine",
    )(dq, dkr, lat, dw)


def unpack_kernel(msg_ref, q_ref, kr_ref, lat_ref, wk_ref, wv_ref):
    ropes = []
    wk = []
    wv = []
    lat = jnp.zeros((TOK, HD), f32)
    for h in range(CTX):
        q_ref[:, h * HD:(h + 1) * HD] = msg_ref[h, 0:TOK, :]
        ropes.append(msg_ref[h, K0:K0 + RD, :].astype(f32))
        lat = lat + msg_ref[h, G0:G0 + TOK, :].astype(f32)
        tail = msg_ref[h, W0:MSG, :].astype(f32)
        wv.append(tail[0:ROWS])
        wk.append(tail[ROWS:2 * ROWS, RD:])
    kr_ref[...] = jnp.concatenate(ropes, 0).T.astype(bf16)
    lat_ref[...] = lat.astype(bf16)
    wk_ref[...] = jnp.concatenate(wk, 1).astype(bf16)
    wv_ref[...] = jnp.concatenate(wv, 1).astype(bf16)


def unpack(msg):
    return pl.pallas_call(
        unpack_kernel,
        out_shape=[
            jax.ShapeDtypeStruct((TOK, CTX * HD), bf16),
            jax.ShapeDtypeStruct((TOK, CTX * RD), bf16),
            jax.ShapeDtypeStruct((TOK, HD), bf16),
            jax.ShapeDtypeStruct((ROWS, CTX * NOPE), bf16),
            jax.ShapeDtypeStruct((ROWS, CTX * HD), bf16),
        ],
        name="unpack",
    )(msg)


def body(latent, key_rope, query, out_grad, positions, freq_index, up_key, up_value):
    ctx = ("zh", "y")
    zh = lax.axis_index("zh")
    head = lax.axis_index(ctx)
    own_freq = lax.dynamic_index_in_dim(freq_index, head, 0, keepdims=False)
    inverse = rope_base ** (-2.0 * own_freq.astype(f32) / HD)

    other = lax.ppermute(latent[0], "zh", [(0, 1), (1, 0)])
    lat = lax.all_gather(jnp.stack([latent[0], other]), "y", axis=0)

    msg = pack(query[0], out_grad[0], key_rope[0], up_key, up_value, positions)
    msg = lax.all_to_all(msg, ctx, 0, 0)

    own_w = msg[:, W0:W0 + 2 * ROWS, :].reshape(CTX, 2, ROWS, HD).transpose(1, 0, 2, 3)
    own_w = own_w.reshape(1, 2 * 32, HD)
    w = lax.all_to_all(jnp.broadcast_to(own_w, (ZL, 2 * 32, HD)), "zl", 0, 0)
    w = lax.all_gather(w, "core", axis=0)

    dq, dkr, dlat, dw = attention(
        zh.reshape(1).astype(jnp.int32), inverse.reshape(HALF_RD, 1), msg, lat, w
    )

    dw = lax.all_to_all(dw, "core", 0, 0)
    dw = (dw[0].astype(f32) + dw[1].astype(f32)).astype(bf16)
    dw = lax.all_to_all(dw, "zl", 0, 0)
    dlat = lax.all_to_all(dlat, "x", 0, 0)
    back = lax.all_to_all(combine(dq, dkr, dlat, dw), ctx, 0, 0)
    query_grad, key_rope_grad, quarter, up_key_grad, up_value_grad = unpack(back)
    latent_grad = lax.all_gather(quarter, "x", axis=1, tiled=True)
    return (query_grad[None], key_rope_grad[None], latent_grad[None], up_key_grad, up_value_grad)


def solution(mesh):
    split = Mesh(mesh.devices.reshape(ZL, CORE, 2, 4, TEN), ("zl", "core", "zh", "y", "x"))
    dp, context, tensor = ("zl", "core"), ("zh", "y"), "x"
    return jax.shard_map(
        body,
        mesh=split,
        in_specs=(
            P(dp, context, None),
            P(dp, context, tensor),
            P(dp, context, tensor),
            P(dp, context, tensor),
            P(dp, context),
            P(tensor, None),
            P(dp + context, tensor),
            P(dp + context, tensor),
        ),
        out_specs=(
            P(dp, context, tensor),
            P(dp, context, tensor),
            P(dp, context, None),
            P(dp + context, tensor),
            P(dp + context, tensor),
        ),
        check_vma=False,
    )
```

```python
import jax
import jax.numpy as jnp
from jax import lax
from jax.experimental import pallas as pl
from jax.experimental.pallas import tpu as pltpu
from jax.sharding import Mesh, PartitionSpec as P

rope_base = 500000.0
neg_large = -1e30
log2_e = 1.4426950408889634

NY = 4
GRP = 2
TOK = 128
HALF = NY * TOK
SEQ = 2 * HALF
HD = 128
RD = 32
HALF_RD = 16
NOPE = 96
RANK = 512
ROWS = 4
ZL = 8
CORE = 2
NZ = 2 * ZL
TEN = 4
Q0, G0, K0, S0, W0, MSG = 0, 256, 512, 576, 592, 608
BL0, BK0, BW0, BACK = 256, 512, 576, 592
BLK = 256

f32 = jnp.float32
bf16 = jnp.bfloat16


def dot(a, b, dims=((1,), (0,))):
    return lax.dot_general(a, b, (dims, ((), ())), preferred_element_type=f32)


def pack_kernel(q_ref, g_ref, kr_ref, wk_ref, wv_ref, pos_ref, out_ref):
    rope_t = kr_ref[...].astype(f32).T.astype(bf16)
    pos = pos_ref[...]
    places = jnp.concatenate(
        [(pos >> 6).astype(f32), (pos & 63).astype(f32), jnp.zeros((14, TOK), f32)], 0
    ).astype(bf16)
    wk = wk_ref[...].astype(f32)
    wv = wv_ref[...].astype(f32)
    for y in range(NY):
        parts_k = []
        parts_v = []
        for g in range(GRP):
            h = y * GRP + g
            cols = slice(h * HD, (h + 1) * HD)
            out_ref[y, Q0 + g * TOK:Q0 + (g + 1) * TOK, :] = q_ref[:, cols]
            out_ref[y, G0 + g * TOK:G0 + (g + 1) * TOK, :] = g_ref[:, cols]
            parts_v.append(wv[:, cols])
            parts_k.append(
                jnp.concatenate([jnp.zeros((ROWS, RD), f32), wk[:, h * NOPE:(h + 1) * NOPE]], 1)
            )
        out_ref[y, K0:S0, :] = rope_t[y * GRP * RD:(y + 1) * GRP * RD, :]
        out_ref[y, S0:W0, :] = places
        out_ref[y, W0:MSG, :] = jnp.concatenate(parts_k + parts_v, 0).astype(bf16)


def pack(query, out_grad, key_rope, up_key, up_value, positions):
    return pl.pallas_call(
        pack_kernel,
        out_shape=jax.ShapeDtypeStruct((NY, MSG, HD), bf16),
        name="pack",
    )(query, out_grad, key_rope, up_key, up_value, positions)


def main_kernel(
    where_ref, inv_ref, msg_ref, other_ref, lat_ref, w_ref,
    dq_ref, dkr_own_ref, dkr_other_ref, dl0_ref, dl1_ref, dl2_ref, dl3_ref, dw_own_ref, dw_other_ref,
    lat_s, w_s, k_s, kt_s, q_s, qt_s, v_s, gt_s, pos_s, cos_s, sin_s, dkv_s, dqt_s, dw_s,
):
    core = where_ref[0]
    x = where_ref[1]
    for z in range(2):
        for y in range(NY):
            c = z * NY + y
            lat_s[c * TOK:(c + 1) * TOK, :] = lat_ref[y, z]
    for z in range(NZ):
        for c in range(CORE):
            r = ((z // 2) * CORE + c) * 32 + (z % 2) * 16
            for kind in range(2 * GRP):
                w_s[r:r + 16, kind * HD:(kind + 1) * HD] = w_ref[c, z, kind * 16:(kind + 1) * 16, :]
    ropes = []
    for z in range(2):
        for y in range(NY):
            c = z * NY + y
            if z == 0:
                tail = msg_ref[y, S0:W0, :].astype(f32)
                ropes.append(msg_ref[y, K0:S0, :])
            else:
                tail = other_ref[y, GRP * RD:GRP * RD + 16, :].astype(f32)
                ropes.append(other_ref[y, 0:GRP * RD, :])
            pos_s[0:1, c * TOK:(c + 1) * TOK] = tail[0:1] * 64.0 + tail[1:2]
    rope_t = jnp.concatenate(ropes, 1).astype(f32)
    pos_row = pos_s[0:1, :]
    angles = inv_ref[...] * pos_row
    cos_s[...] = jnp.cos(angles)
    sin_s[...] = jnp.sin(angles)
    pos_col = jnp.broadcast_to(pos_row, (8, SEQ)).T[:, 0:1]
    scale = HD ** -0.5
    kv = dot(lat_s[...], w_s[...])
    dkv_s[...] = jnp.zeros_like(dkv_s)

    for g in range(GRP):
        cos = cos_s[g * HALF_RD:(g + 1) * HALF_RD, :]
        sin = sin_s[g * HALF_RD:(g + 1) * HALF_RD, :]

        def rot(a, width):
            a, b = a[:HALF_RD], a[HALF_RD:RD]
            c, s = cos[:, :width], sin[:, :width]
            return jnp.concatenate([a * c - b * s, b * c + a * s], 0)

        def unrot(a, width):
            a, b = a[:HALF_RD], a[HALF_RD:RD]
            c, s = cos[:, :width], sin[:, :width]
            return jnp.concatenate([a * c + b * s, b * c - a * s], 0)

        kr = rot(rope_t[g * RD:(g + 1) * RD, :], SEQ)
        kr_pad = jnp.concatenate([kr, jnp.zeros((HD - RD, SEQ), f32)], 0)
        k = kv[:, g * HD:(g + 1) * HD] + kr_pad.T
        k_s[...] = k.astype(bf16)
        kt_s[...] = k.T.astype(bf16)
        v_s[...] = kv[:, (GRP + g) * HD:(GRP + g + 1) * HD].astype(bf16)
        for c in range(NY):
            cols = slice(c * TOK, (c + 1) * TOK)
            qt_s[:, cols] = msg_ref[c, Q0 + g * TOK:Q0 + (g + 1) * TOK, :].astype(f32).T
            gt_s[:, cols] = msg_ref[c, G0 + g * TOK:G0 + (g + 1) * TOK, :].astype(f32).T.astype(bf16)
        qt_s[0:RD, :] = rot(qt_s[0:RD, :], HALF)
        qt = qt_s[...]
        q_s[...] = qt.T.astype(bf16)

        for b in range(HALF // BLK):
            cols = slice(b * BLK, (b + 1) * BLK)
            st = dot(k_s[...], qt[:, cols].astype(bf16))
            visible = pos_col <= pos_row[:, cols]
            st = jnp.where(visible, st * (scale * log2_e), neg_large)
            top = jnp.max(st, 0, keepdims=True)
            e = jnp.exp2(st - top)
            dp = dot(v_s[...], gt_s[:, cols])
            total = jnp.sum(e, 0, keepdims=True)
            weighted = jnp.sum(e * dp, 0, keepdims=True)
            inv_total = 1.0 / total
            delta = weighted * inv_total
            probs = (e * inv_total).astype(bf16)
            ds = (scale * probs.astype(f32) * (dp - delta)).astype(bf16)
            dqt_s[:, cols] = dot(kt_s[...], ds)
            dkv_s[:, g * HD:(g + 1) * HD] += dot(ds, q_s[cols, :])
            grad = jnp.concatenate(
                [
                    msg_ref[c, G0 + g * TOK:G0 + (g + 1) * TOK, :]
                    for c in range(b * BLK // TOK, (b + 1) * BLK // TOK)
                ],
                0,
            )
            dkv_s[:, (GRP + g) * HD:(GRP + g + 1) * HD] += dot(probs, grad)

        dqt_s[0:RD, :] = unrot(dqt_s[0:RD, :], HALF)
        dq = dqt_s[...].T.astype(bf16)
        dkr = unrot(dkv_s[:, g * HD:(g + 1) * HD].T[0:RD, :], SEQ).astype(bf16)
        for c in range(NY):
            cols = slice(c * TOK, (c + 1) * TOK)
            dq_ref[c, g * TOK:(g + 1) * TOK, :] = dq[cols, :]
            dkr_own_ref[c, g * RD:(g + 1) * RD, :] = dkr[:, cols]
            dkr_other_ref[c, g * RD:(g + 1) * RD, :] = dkr[:, HALF + c * TOK:HALF + (c + 1) * TOK]

    dkv = dkv_s[...].astype(bf16)
    for t, ref in enumerate((dl0_ref, dl1_ref, dl2_ref, dl3_ref)):
        rows = pl.ds(pl.multiple_of((x ^ t) * HD, HD), HD)
        ref[...] = dot(dkv, w_s[rows, :], ((1,), (1,))).astype(bf16)
    dw_s[...] = dot(lat_s[...], dkv, ((0,), (0,)))
    for z in range(NZ):
        base = (z // 2) * CORE * 32 + (z % 2) * 16
        dw_own_ref[z] = dw_s[pl.ds(pl.multiple_of(base + core * 32, 16), 16), :].astype(bf16)
        dw_other_ref[z] = dw_s[pl.ds(pl.multiple_of(base + (1 - core) * 32, 16), 16), :].astype(bf16)


def attention(place, inverse, msg, other, lat, w):
    smem = pl.BlockSpec(memory_space=pltpu.SMEM)
    vmem = pl.BlockSpec(memory_space=pltpu.VMEM)
    rope = jax.ShapeDtypeStruct((NY, GRP * RD, TOK), bf16)
    quarter = jax.ShapeDtypeStruct((SEQ, HD), bf16)
    weight = jax.ShapeDtypeStruct((NZ, 16, 2 * GRP * HD), bf16)
    return pl.pallas_call(
        main_kernel,
        in_specs=[smem] + [vmem] * 5,
        out_specs=[vmem] * 9,
        out_shape=[jax.ShapeDtypeStruct((NY, GRP * TOK, HD), bf16), rope, rope]
        + [quarter] * 4
        + [weight, weight],
        scratch_shapes=[
            pltpu.VMEM((SEQ, RANK), bf16),
            pltpu.VMEM((RANK, 2 * GRP * HD), bf16),
            pltpu.VMEM((SEQ, HD), bf16),
            pltpu.VMEM((HD, SEQ), bf16),
            pltpu.VMEM((HALF, HD), bf16),
            pltpu.VMEM((HD, HALF), f32),
            pltpu.VMEM((SEQ, HD), bf16),
            pltpu.VMEM((HD, HALF), bf16),
            pltpu.VMEM((8, SEQ), f32),
            pltpu.VMEM((GRP * HALF_RD, SEQ), f32),
            pltpu.VMEM((GRP * HALF_RD, SEQ), f32),
            pltpu.VMEM((SEQ, 2 * GRP * HD), f32),
            pltpu.VMEM((HD, HALF), f32),
            pltpu.VMEM((RANK, 2 * GRP * HD), f32),
        ],
        compiler_params=pltpu.CompilerParams(vmem_limit_bytes=56 * 1024 * 1024),
        name="attention_backward",
    )(place, inverse, msg, other, lat, w)


def combine_kernel(dq_ref, kr0_ref, kr1_ref, l0_ref, l1_ref, l2_ref, l3_ref, dw_ref, out_ref):
    dw = jnp.sum(dw_ref[...].astype(f32), 0)
    for y in range(NY):
        out_ref[y, 0:BL0, :] = dq_ref[y]
        out_ref[y, BK0:BW0, :] = (kr0_ref[y].astype(f32) + kr1_ref[y].astype(f32)).astype(bf16)
        for z in range(2):
            rows = slice((z * NY + y) * TOK, (z * NY + y + 1) * TOK)
            lat = (l0_ref[rows, :].astype(f32) + l1_ref[rows, :].astype(f32)) + (
                l2_ref[rows, :].astype(f32) + l3_ref[rows, :].astype(f32)
            )
            out_ref[y, BL0 + z * TOK:BL0 + (z + 1) * TOK, :] = lat.astype(bf16)
        part = dw[y * ROWS:(y + 1) * ROWS, :]
        out_ref[y, BW0:BACK, :] = jnp.concatenate(
            [part[:, c * HD:(c + 1) * HD] for c in range(2 * GRP)], 0
        ).astype(bf16)


def combine(*parts):
    return pl.pallas_call(
        combine_kernel,
        out_shape=jax.ShapeDtypeStruct((NY, BACK, HD), bf16),
        name="combine",
    )(*parts)


def unpack_kernel(where_ref, msg_ref, q_ref, kr_ref, lat_ref, wk_ref, wv_ref):
    half = where_ref[0]
    ropes = []
    wk = []
    wv = []
    for y in range(NY):
        for g in range(GRP):
            h = y * GRP + g
            q_ref[:, h * HD:(h + 1) * HD] = msg_ref[y, g * TOK:(g + 1) * TOK, :]
        ropes.append(msg_ref[y, BK0:BW0, :].astype(f32))
        tail = msg_ref[y, BW0:BACK, :].astype(f32)
        for g in range(GRP):
            wk.append(tail[g * ROWS:(g + 1) * ROWS, RD:])
            wv.append(tail[(GRP + g) * ROWS:(GRP + g + 1) * ROWS])
    for z in range(2):
        lat = sum(
            msg_ref[y, BL0 + z * TOK:BL0 + (z + 1) * TOK, :].astype(f32) for y in range(NY)
        ).astype(bf16)
        for t in range(TEN):
            lat_ref[z ^ half, t] = lat
    kr_ref[...] = jnp.concatenate(ropes, 0).T.astype(bf16)
    wk_ref[...] = jnp.concatenate(wk, 1).astype(bf16)
    wv_ref[...] = jnp.concatenate(wv, 1).astype(bf16)


def unpack(half, msg):
    return pl.pallas_call(
        unpack_kernel,
        in_specs=[
            pl.BlockSpec(memory_space=pltpu.SMEM),
            pl.BlockSpec(memory_space=pltpu.VMEM),
        ],
        out_shape=[
            jax.ShapeDtypeStruct((TOK, NY * GRP * HD), bf16),
            jax.ShapeDtypeStruct((TOK, NY * GRP * RD), bf16),
            jax.ShapeDtypeStruct((2, TEN, TOK, HD), bf16),
            jax.ShapeDtypeStruct((ROWS, NY * GRP * NOPE), bf16),
            jax.ShapeDtypeStruct((ROWS, NY * GRP * HD), bf16),
        ],
        name="unpack",
    )(half, msg)


def swap(array, axis, size, flip):
    return lax.ppermute(array, axis, [(i, i ^ flip) for i in range(size)])


def body(latent, key_rope, query, out_grad, positions, freq_index, up_key, up_value):
    i32 = jnp.int32
    zh = lax.axis_index("zh").astype(i32)
    y = lax.axis_index("y")
    place = jnp.stack([lax.axis_index("core").astype(i32), lax.axis_index("x").astype(i32)])
    own_freq = lax.dynamic_slice_in_dim(freq_index, y * GRP, GRP, 0)
    inverse = rope_base ** (-2.0 * own_freq.astype(f32) / HD)

    other_lat = swap(latent[0], "zh", 2, 1)
    lat = lax.all_gather(jnp.stack([latent[0], other_lat]), "y", axis=0)

    msg = pack(query[0], out_grad[0], key_rope[0], up_key, up_value, positions)
    msg = lax.all_to_all(msg, "y", 0, 0)
    other = swap(msg[:, K0:W0, :], "zh", 2, 1)

    own_w = msg[:, W0:MSG, :].reshape(NY, 2 * GRP, ROWS, HD).transpose(1, 0, 2, 3)
    own_w = own_w.reshape(1, 2 * GRP * NY * ROWS, HD)
    w = lax.all_to_all(jnp.broadcast_to(own_w, (NZ,) + own_w.shape[1:]), ("zl", "zh"), 0, 0)
    w = lax.all_gather(w, "core", axis=0)

    dq, kr_own, kr_other, l0, l1, l2, l3, dw_own, dw_other = attention(
        place, inverse.reshape(GRP * HALF_RD, 1), msg, other, lat, w
    )

    dw = dw_own.astype(f32) + swap(dw_other, "core", 2, 1).astype(f32)
    dw = lax.all_to_all(dw.astype(bf16), ("zl", "zh"), 0, 0)
    l1 = swap(l1, "x", TEN, 1)
    l2 = swap(l2, "x", TEN, 2)
    l3 = swap(l3, "x", TEN, 3)
    kr_other = swap(kr_other, "zh", 2, 1)
    back = lax.all_to_all(combine(dq, kr_own, kr_other, l0, l1, l2, l3, dw), "y", 0, 0)
    query_grad, key_rope_grad, quarters, up_key_grad, up_value_grad = unpack(zh.reshape(1), back)
    quarters = lax.all_to_all(quarters.reshape(2 * TEN, TOK, HD), ("zh", "x"), 0, 0)
    halves = quarters.reshape(2, TEN, TOK, HD).astype(f32)
    latent_grad = (halves[0] + halves[1]).astype(bf16).transpose(1, 0, 2).reshape(1, TOK, RANK)
    return (query_grad[None], key_rope_grad[None], latent_grad, up_key_grad, up_value_grad)


def solution(mesh):
    split = Mesh(mesh.devices.reshape(ZL, CORE, 2, NY, TEN), ("zl", "core", "zh", "y", "x"))
    dp, context, tensor = ("zl", "core"), ("zh", "y"), "x"
    return jax.shard_map(
        body,
        mesh=split,
        in_specs=(
            P(dp, context, None),
            P(dp, context, tensor),
            P(dp, context, tensor),
            P(dp, context, tensor),
            P(dp, context),
            P(tensor, None),
            P(dp + context, tensor),
            P(dp + context, tensor),
        ),
        out_specs=(
            P(dp, context, tensor),
            P(dp, context, tensor),
            P(dp, context, None),
            P(dp + context, tensor),
            P(dp + context, tensor),
        ),
        check_vma=False,
    )
```

```python
import math

import jax
import jax.numpy as jnp
from jax import lax
from jax.experimental import pallas as pl
from jax.experimental.pallas import tpu as pltpu
from jax.sharding import Mesh, PartitionSpec as P

rope_base = 500000.0
neg_large = -1e30
log2_e = 1.4426950408889634

NY = 4
GRP = 2
TOK = 128
HALF = NY * TOK
SEQ = 2 * HALF
HD = 128
RD = 32
HALF_RD = 16
NOPE = 96
RANK = 512
ROWS = 4
ZL = 8
CORE = 2
NZ = 2 * ZL
TEN = 4
Q0, G0, L0, K0, S0, W0, MSG = 0, 256, 512, 1024, 1088, 1104, 1120
KEY_K, KEY_S, KEY = 512, 768, 784
PASS_S, PASS = 576, 592
BL0, BK0, BW0, BACK = 256, 512, 640, 672
EK0, EW0, END = 128, 384, 448
BLK = 256

f32 = jnp.float32
bf16 = jnp.bfloat16


def dot(a, b, dims=((1,), (0,))):
    return lax.dot_general(a, b, (dims, ((), ())), preferred_element_type=f32)


def pack_kernel(q_ref, g_ref, kr_ref, lat_ref, wk_ref, wv_ref, pos_ref, out_ref, key_ref):
    rope_t = kr_ref[...].astype(f32).T.astype(bf16)
    pos = pos_ref[...]
    places = jnp.concatenate(
        [(pos >> 6).astype(f32), (pos & 63).astype(f32), jnp.zeros((14, TOK), f32)], 0
    ).astype(bf16)
    for b in range(RANK // HD):
        key_ref[b * TOK:(b + 1) * TOK, :] = lat_ref[:, b * HD:(b + 1) * HD]
    key_ref[KEY_K:KEY_S, :] = rope_t
    key_ref[KEY_S:KEY, :] = places
    wk = wk_ref[...].astype(f32)
    wv = wv_ref[...].astype(f32)
    for y in range(NY):
        parts_k = []
        parts_v = []
        for g in range(GRP):
            h = y * GRP + g
            cols = slice(h * HD, (h + 1) * HD)
            out_ref[y, Q0 + g * TOK:Q0 + (g + 1) * TOK, :] = q_ref[:, cols]
            out_ref[y, G0 + g * TOK:G0 + (g + 1) * TOK, :] = g_ref[:, cols]
            parts_v.append(wv[:, cols])
            parts_k.append(
                jnp.concatenate([jnp.zeros((ROWS, RD), f32), wk[:, h * NOPE:(h + 1) * NOPE]], 1)
            )
        for b in range(RANK // HD):
            out_ref[y, L0 + b * TOK:L0 + (b + 1) * TOK, :] = lat_ref[:, b * HD:(b + 1) * HD]
        out_ref[y, K0:S0, :] = rope_t[y * GRP * RD:(y + 1) * GRP * RD, :]
        out_ref[y, S0:W0, :] = places
        out_ref[y, W0:MSG, :] = jnp.concatenate(parts_k + parts_v, 0).astype(bf16)


def pack(*parts):
    return pl.pallas_call(
        pack_kernel,
        out_shape=[
            jax.ShapeDtypeStruct((NY, MSG, HD), bf16),
            jax.ShapeDtypeStruct((KEY, HD), bf16),
        ],
        name="pack",
    )(*parts)


def spread_kernel(msg_ref, w_ref):
    tails = [msg_ref[y].astype(f32) for y in range(NY)]
    rows = [tails[y][c * ROWS:(c + 1) * ROWS] for c in range(2 * GRP) for y in range(NY)]
    block = jnp.concatenate(rows, 0).astype(bf16)
    for z in range(NZ):
        w_ref[z] = block


def spread(msg):
    return pl.pallas_call(
        spread_kernel,
        grid=(1,),
        in_specs=[pl.BlockSpec((NY, MSG - W0, HD), lambda i: (0, W0 // (MSG - W0), 0))],
        out_specs=pl.BlockSpec(memory_space=pltpu.VMEM),
        out_shape=jax.ShapeDtypeStruct((NZ, 2 * GRP * NY * ROWS, HD), bf16),
        name="spread",
    )(msg)


def relay_kernel(where_ref, key_ref, *out_refs):
    own_y = where_ref[2]
    for t, ref in enumerate(out_refs):
        rows = KEY_K + (own_y ^ t) * (GRP * RD)
        ref[0:KEY_K, :] = key_ref[0:KEY_K, :]
        ref[KEY_K:PASS_S, :] = key_ref[pl.ds(pl.multiple_of(rows, GRP * RD), GRP * RD), :]
        ref[PASS_S:PASS, :] = key_ref[KEY_S:KEY, :]


def relay(place, other):
    return pl.pallas_call(
        relay_kernel,
        in_specs=[
            pl.BlockSpec(memory_space=pltpu.SMEM),
            pl.BlockSpec(memory_space=pltpu.VMEM),
        ],
        out_shape=[jax.ShapeDtypeStruct((PASS, HD), bf16)] * NY,
        cost_estimate=pl.CostEstimate(flops=50_000_000_000, transcendentals=0, bytes_accessed=150_000_000),
        name="relay",
    )(place, other)


def main_kernel(
    where_ref, freq_ref, msg_ref, key0_ref, key1_ref, key2_ref, key3_ref, w_ref,
    dq_ref, dkr_ref, dl0_ref, dl1_ref, dl2_ref, dl3_ref, dw_own_ref, dw_other_ref,
    lat_s, w_s, k_s, kt_s, q_s, qt_s, v_s, gt_s, pos_s, rope_s, cos_s, sin_s, dkv_s, dqt_s, dw_s,
):
    core = where_ref[0]
    x = where_ref[1]
    own_y = where_ref[2]
    def take(read, lat0, rope0, pos0, tokens):
        for b in range(RANK // HD):
            lat_s[tokens, b * HD:(b + 1) * HD] = read(lat0 + b * TOK, TOK)
        rope_s[:, tokens] = read(rope0, GRP * RD).astype(f32)
        tail = read(pos0, 16).astype(f32)
        pos_s[0:1, tokens] = tail[0:1] * 64.0 + tail[1:2]

    for y in range(NY):
        take(
            lambda r, n, y=y: msg_ref[y, r:r + n, :], L0, K0, S0,
            slice(y * TOK, (y + 1) * TOK),
        )
    for t, ref in enumerate((key0_ref, key1_ref, key2_ref, key3_ref)):
        tokens = pl.ds(pl.multiple_of((NY + (own_y ^ t)) * TOK, TOK), TOK)
        take(lambda r, n, ref=ref: ref[r:r + n, :], 0, KEY_K, PASS_S, tokens)
    for z in range(NZ):
        for c in range(CORE):
            r = ((z // 2) * CORE + c) * 32 + (z % 2) * 16
            for kind in range(2 * GRP):
                w_s[r:r + 16, kind * HD:(kind + 1) * HD] = w_ref[c, z, kind * 16:(kind + 1) * 16, :]
    pos_row = pos_s[0:1, :]
    freq = freq_ref[...].astype(f32)
    heads = lax.broadcasted_iota(jnp.int32, freq.shape, 0)
    diagonal = lax.broadcasted_iota(jnp.int32, (HALF_RD, HALF_RD), 0) == lax.broadcasted_iota(
        jnp.int32, (HALF_RD, HALF_RD), 1
    )
    columns = []
    for g in range(GRP):
        row = jnp.sum(jnp.where(heads == own_y * GRP + g, freq, 0.0), 0, keepdims=True)
        columns.append(jnp.sum(jnp.where(diagonal, row, 0.0), 1, keepdims=True))
    inverse = jnp.exp(jnp.concatenate(columns, 0) * (-2.0 / HD * math.log(rope_base)))
    angles = inverse * pos_row
    cos_s[...] = jnp.cos(angles)
    sin_s[...] = jnp.sin(angles)
    pos_col = jnp.broadcast_to(pos_row, (8, SEQ)).T[:, 0:1]
    scale = HD ** -0.5
    kv = dot(lat_s[...], w_s[...])
    dkv_s[...] = jnp.zeros_like(dkv_s)

    for g in range(GRP):
        cos = cos_s[g * HALF_RD:(g + 1) * HALF_RD, :]
        sin = sin_s[g * HALF_RD:(g + 1) * HALF_RD, :]

        def rot(a, width):
            a, b = a[:HALF_RD], a[HALF_RD:RD]
            c, s = cos[:, :width], sin[:, :width]
            return jnp.concatenate([a * c - b * s, b * c + a * s], 0)

        def unrot(a, width):
            a, b = a[:HALF_RD], a[HALF_RD:RD]
            c, s = cos[:, :width], sin[:, :width]
            return jnp.concatenate([a * c + b * s, b * c - a * s], 0)

        kr = rot(rope_s[g * RD:(g + 1) * RD, :], SEQ)
        kr_pad = jnp.concatenate([kr, jnp.zeros((HD - RD, SEQ), f32)], 0)
        k = kv[:, g * HD:(g + 1) * HD] + kr_pad.T
        k_s[...] = k.astype(bf16)
        kt_s[...] = k.T.astype(bf16)
        v_s[...] = kv[:, (GRP + g) * HD:(GRP + g + 1) * HD].astype(bf16)
        for c in range(NY):
            cols = slice(c * TOK, (c + 1) * TOK)
            qt_s[:, cols] = msg_ref[c, Q0 + g * TOK:Q0 + (g + 1) * TOK, :].astype(f32).T
            gt_s[:, cols] = msg_ref[c, G0 + g * TOK:G0 + (g + 1) * TOK, :].astype(f32).T.astype(bf16)
        qt_s[0:RD, :] = rot(qt_s[0:RD, :], HALF)
        qt = qt_s[...]
        q_s[...] = qt.T.astype(bf16)

        for b in range(HALF // BLK):
            cols = slice(b * BLK, (b + 1) * BLK)
            st = dot(k_s[...], qt[:, cols].astype(bf16))
            visible = pos_col <= pos_row[:, cols]
            st = jnp.where(visible, st * (scale * log2_e), neg_large)
            top = jnp.max(st, 0, keepdims=True)
            e = jnp.exp2(st - top)
            dp = dot(v_s[...], gt_s[:, cols])
            total = jnp.sum(e, 0, keepdims=True)
            weighted = jnp.sum(e * dp, 0, keepdims=True)
            inv_total = 1.0 / total
            delta = weighted * inv_total
            probs = (e * inv_total).astype(bf16)
            ds = (scale * probs.astype(f32) * (dp - delta)).astype(bf16)
            dqt_s[:, cols] = dot(kt_s[...], ds)
            dkv_s[:, g * HD:(g + 1) * HD] += dot(ds, q_s[cols, :])
            grad = jnp.concatenate(
                [
                    msg_ref[c, G0 + g * TOK:G0 + (g + 1) * TOK, :]
                    for c in range(b * BLK // TOK, (b + 1) * BLK // TOK)
                ],
                0,
            )
            dkv_s[:, (GRP + g) * HD:(GRP + g + 1) * HD] += dot(probs, grad)

        dqt_s[0:RD, :] = unrot(dqt_s[0:RD, :], HALF)
        dq = dqt_s[...].T.astype(bf16)
        dkr = unrot(dkv_s[:, g * HD:(g + 1) * HD].T[0:RD, :], SEQ).astype(bf16)
        for c in range(NY):
            cols = slice(c * TOK, (c + 1) * TOK)
            dq_ref[c, g * TOK:(g + 1) * TOK, :] = dq[cols, :]
            for z in range(2):
                rows = slice((z * GRP + g) * RD, (z * GRP + g + 1) * RD)
                dkr_ref[c, rows, :] = dkr[:, z * HALF + c * TOK:z * HALF + (c + 1) * TOK]

    dkv = dkv_s[...].astype(bf16)
    for t, ref in enumerate((dl0_ref, dl1_ref, dl2_ref, dl3_ref)):
        rows = pl.ds(pl.multiple_of((x ^ t) * HD, HD), HD)
        ref[...] = dot(dkv, w_s[rows, :], ((1,), (1,))).astype(bf16)
    dw_s[...] = dot(lat_s[...], dkv, ((0,), (0,)))
    for z in range(ZL):
        own = pl.ds(pl.multiple_of((z * CORE + core) * 32, 32), 32)
        other = pl.ds(pl.multiple_of((z * CORE + 1 - core) * 32, 32), 32)
        dw_own_ref[z] = dw_s[own, :].astype(bf16)
        dw_other_ref[z] = dw_s[other, :].astype(bf16)


def attention(place, freq, msg, keys, w):
    smem = pl.BlockSpec(memory_space=pltpu.SMEM)
    vmem = pl.BlockSpec(memory_space=pltpu.VMEM)
    rope = jax.ShapeDtypeStruct((NY, 2 * GRP * RD, TOK), bf16)
    quarter = jax.ShapeDtypeStruct((SEQ, HD), bf16)
    weight = jax.ShapeDtypeStruct((ZL, 32, 2 * GRP * HD), bf16)
    return pl.pallas_call(
        main_kernel,
        in_specs=[smem] + [vmem] * 7,
        out_specs=[vmem] * 8,
        out_shape=[jax.ShapeDtypeStruct((NY, GRP * TOK, HD), bf16), rope]
        + [quarter] * 4
        + [weight, weight],
        scratch_shapes=[
            pltpu.VMEM((SEQ, RANK), bf16),
            pltpu.VMEM((RANK, 2 * GRP * HD), bf16),
            pltpu.VMEM((SEQ, HD), bf16),
            pltpu.VMEM((HD, SEQ), bf16),
            pltpu.VMEM((HALF, HD), bf16),
            pltpu.VMEM((HD, HALF), f32),
            pltpu.VMEM((SEQ, HD), bf16),
            pltpu.VMEM((HD, HALF), bf16),
            pltpu.VMEM((8, SEQ), f32),
            pltpu.VMEM((GRP * RD, SEQ), f32),
            pltpu.VMEM((GRP * HALF_RD, SEQ), f32),
            pltpu.VMEM((GRP * HALF_RD, SEQ), f32),
            pltpu.VMEM((SEQ, 2 * GRP * HD), f32),
            pltpu.VMEM((HD, HALF), f32),
            pltpu.VMEM((RANK, 2 * GRP * HD), f32),
        ],
        compiler_params=pltpu.CompilerParams(vmem_limit_bytes=56 * 1024 * 1024),
        name="attention_backward",
    )(place, freq, msg, *keys, w)


def combine_kernel(dq_ref, kr_ref, l0_ref, l1_ref, l2_ref, l3_ref, dw_ref, out_ref):
    dw = jnp.sum(dw_ref[...].astype(f32), 0)
    for y in range(NY):
        out_ref[y, 0:BL0, :] = dq_ref[y]
        out_ref[y, BK0:BW0, :] = kr_ref[y]
        for z in range(2):
            rows = slice((z * NY + y) * TOK, (z * NY + y + 1) * TOK)
            lat = (l0_ref[rows, :].astype(f32) + l1_ref[rows, :].astype(f32)) + (
                l2_ref[rows, :].astype(f32) + l3_ref[rows, :].astype(f32)
            )
            out_ref[y, BL0 + z * TOK:BL0 + (z + 1) * TOK, :] = lat.astype(bf16)
        for z in range(2):
            part = dw[z * 16 + y * ROWS:z * 16 + (y + 1) * ROWS, :]
            out_ref[y, BW0 + z * 16:BW0 + (z + 1) * 16, :] = jnp.concatenate(
                [part[:, c * HD:(c + 1) * HD] for c in range(2 * GRP)], 0
            ).astype(bf16)


def combine(*parts):
    return pl.pallas_call(
        combine_kernel,
        out_shape=jax.ShapeDtypeStruct((NY, BACK, HD), bf16),
        name="combine",
    )(*parts)


def halves_kernel(where_ref, msg_ref, own_ref, other_ref):
    half = where_ref[3]
    for z, ref in enumerate((own_ref, other_ref)):
        lat = sum(
            msg_ref[y, BL0 + z * TOK:BL0 + (z + 1) * TOK, :].astype(f32) for y in range(NY)
        )
        ref[0:TOK, :] = lat.astype(bf16)
        weights = pl.ds(pl.multiple_of(BW0 + (half ^ z) * 16, 16), 16)
        for y in range(NY):
            rows = slice(EK0 + y * GRP * RD, EK0 + (y + 1) * GRP * RD)
            ref[rows, :] = msg_ref[y, BK0 + z * GRP * RD:BK0 + (z + 1) * GRP * RD, :]
            ref[EW0 + y * 16:EW0 + (y + 1) * 16, :] = msg_ref[y, weights, :]


def halves(place, msg):
    part = jax.ShapeDtypeStruct((END, HD), bf16)
    return pl.pallas_call(
        halves_kernel,
        in_specs=[
            pl.BlockSpec(memory_space=pltpu.SMEM),
            pl.BlockSpec(memory_space=pltpu.VMEM),
        ],
        out_shape=[part, part],
        name="halves",
    )(place, msg)


def unpack_kernel(msg_ref, q_ref):
    for y in range(NY):
        for g in range(GRP):
            h = y * GRP + g
            q_ref[:, h * HD:(h + 1) * HD] = msg_ref[y, g * TOK:(g + 1) * TOK, :]


def unpack(msg):
    return pl.pallas_call(
        unpack_kernel,
        out_shape=jax.ShapeDtypeStruct((TOK, NY * GRP * HD), bf16),
        name="unpack",
    )(msg)


def finish_kernel(own_ref, other_ref, lat_ref, kr_ref, wk_ref, wv_ref):
    both = own_ref[...].astype(f32) + other_ref[...].astype(f32)
    lat = both[0:TOK].astype(bf16)
    for t in range(TEN):
        lat_ref[t] = lat
    kr_ref[...] = both[EK0:EW0].T.astype(bf16)
    wk = []
    wv = []
    for y in range(NY):
        tail = both[EW0 + y * 16:EW0 + (y + 1) * 16]
        for g in range(GRP):
            wk.append(tail[g * ROWS:(g + 1) * ROWS, RD:])
            wv.append(tail[(GRP + g) * ROWS:(GRP + g + 1) * ROWS])
    wk_ref[...] = jnp.concatenate(wk, 1).astype(bf16)
    wv_ref[...] = jnp.concatenate(wv, 1).astype(bf16)


def finish(own, other):
    return pl.pallas_call(
        finish_kernel,
        out_shape=[
            jax.ShapeDtypeStruct((TEN, TOK, HD), bf16),
            jax.ShapeDtypeStruct((TOK, NY * GRP * RD), bf16),
            jax.ShapeDtypeStruct((ROWS, NY * GRP * NOPE), bf16),
            jax.ShapeDtypeStruct((ROWS, NY * GRP * HD), bf16),
        ],
        name="finish",
    )(own, other)


def swap(array, axis, size, flip):
    return lax.ppermute(array, axis, [(i, i ^ flip) for i in range(size)])


def body(latent, key_rope, query, out_grad, positions, freq_index, up_key, up_value):
    place = jnp.stack([lax.axis_index(a).astype(jnp.int32) for a in ("core", "x", "y", "zh")])

    msg, own = pack(query[0], out_grad[0], key_rope[0], latent[0], up_key, up_value, positions)
    other = swap(own, "zh", 2, 1)
    msg = lax.all_to_all(msg, "y", 0, 0)
    w = lax.all_to_all(spread(msg), ("zl", "zh"), 0, 0)
    keys = relay(place, other)
    keys = [keys[0]] + [swap(keys[t], "y", NY, t) for t in range(1, NY)]
    w = lax.all_gather(w, "core", axis=0)

    dq, dkr, l0, l1, l2, l3, dw_own, dw_other = attention(place, freq_index, msg, keys, w)

    dw = dw_own.astype(f32) + swap(dw_other, "core", 2, 1).astype(f32)
    dw = lax.all_to_all(dw.astype(bf16), "zl", 0, 0)
    l1 = swap(l1, "x", TEN, 1)
    l2 = swap(l2, "x", TEN, 2)
    l3 = swap(l3, "x", TEN, 3)
    back = lax.all_to_all(combine(dq, dkr, l0, l1, l2, l3, dw), "y", 0, 0)
    own, other = halves(place, back)
    quarter, key_rope_grad, up_key_grad, up_value_grad = finish(own, swap(other, "zh", 2, 1))
    query_grad = unpack(back)
    quarters = lax.all_to_all(quarter, "x", 0, 0)
    latent_grad = quarters.transpose(1, 0, 2).reshape(1, TOK, RANK)
    return (query_grad[None], key_rope_grad[None], latent_grad, up_key_grad, up_value_grad)


def solution(mesh):
    split = Mesh(mesh.devices.reshape(ZL, CORE, 2, NY, TEN), ("zl", "core", "zh", "y", "x"))
    dp, context, tensor = ("zl", "core"), ("zh", "y"), "x"
    return jax.shard_map(
        body,
        mesh=split,
        in_specs=(
            P(dp, context, None),
            P(dp, context, tensor),
            P(dp, context, tensor),
            P(dp, context, tensor),
            P(dp, context),
            P(tensor, None),
            P(dp + context, tensor),
            P(dp + context, tensor),
        ),
        out_specs=(
            P(dp, context, tensor),
            P(dp, context, tensor),
            P(dp, context, None),
            P(dp + context, tensor),
            P(dp + context, tensor),
        ),
        check_vma=False,
    )
```

```python
import math

import jax
import jax.numpy as jnp
from jax import lax
from jax.experimental import pallas as pl
from jax.experimental.pallas import tpu as pltpu
from jax.sharding import Mesh, PartitionSpec as P

rope_base = 500000.0
neg_large = -1e30
log2_e = 1.4426950408889634

NY = 4
GRP = 2
TOK = 128
HALF = NY * TOK
SEQ = 2 * HALF
HD = 128
RD = 32
HALF_RD = 16
NOPE = 96
RANK = 512
ROWS = 4
ZL = 8
CORE = 2
NZ = 2 * ZL
TEN = 4
Q0, G0, L0, K0, S0, W0, MSG = 0, 256, 512, 1024, 1088, 1104, 1120
KEY_K, KEY_S, KEY = 512, 768, 784
PASS_S, PASS = 576, 592
BK0, BW0, BACK = 256, 320, 336
BLK = 256

waits_for_z = pl.CostEstimate(flops=50_000_000_000, transcendentals=0, bytes_accessed=150_000_000)
f32 = jnp.float32
bf16 = jnp.bfloat16


def dot(a, b, dims=((1,), (0,))):
    return lax.dot_general(a, b, (dims, ((), ())), preferred_element_type=f32)


def pack_kernel(q_ref, g_ref, kr_ref, lat_ref, wk_ref, wv_ref, pos_ref, out_ref, key_ref):
    rope_t = kr_ref[...].astype(f32).T.astype(bf16)
    pos = pos_ref[...]
    places = jnp.concatenate(
        [(pos >> 6).astype(f32), (pos & 63).astype(f32), jnp.zeros((14, TOK), f32)], 0
    ).astype(bf16)
    for b in range(RANK // HD):
        key_ref[b * TOK:(b + 1) * TOK, :] = lat_ref[:, b * HD:(b + 1) * HD]
    key_ref[KEY_K:KEY_S, :] = rope_t
    key_ref[KEY_S:KEY, :] = places
    wk = wk_ref[...].astype(f32)
    wv = wv_ref[...].astype(f32)
    for y in range(NY):
        parts_k = []
        parts_v = []
        for g in range(GRP):
            h = y * GRP + g
            cols = slice(h * HD, (h + 1) * HD)
            out_ref[y, Q0 + g * TOK:Q0 + (g + 1) * TOK, :] = q_ref[:, cols]
            out_ref[y, G0 + g * TOK:G0 + (g + 1) * TOK, :] = g_ref[:, cols]
            parts_v.append(wv[:, cols])
            parts_k.append(
                jnp.concatenate([jnp.zeros((ROWS, RD), f32), wk[:, h * NOPE:(h + 1) * NOPE]], 1)
            )
        for b in range(RANK // HD):
            out_ref[y, L0 + b * TOK:L0 + (b + 1) * TOK, :] = lat_ref[:, b * HD:(b + 1) * HD]
        out_ref[y, K0:S0, :] = rope_t[y * GRP * RD:(y + 1) * GRP * RD, :]
        out_ref[y, S0:W0, :] = places
        out_ref[y, W0:MSG, :] = jnp.concatenate(parts_k + parts_v, 0).astype(bf16)


def pack(*parts):
    return pl.pallas_call(
        pack_kernel,
        out_shape=[
            jax.ShapeDtypeStruct((NY, MSG, HD), bf16),
            jax.ShapeDtypeStruct((KEY, HD), bf16),
        ],
        name="pack",
    )(*parts)


def spread_kernel(msg_ref, w_ref):
    tails = [msg_ref[y].astype(f32) for y in range(NY)]
    rows = [tails[y][c * ROWS:(c + 1) * ROWS] for c in range(2 * GRP) for y in range(NY)]
    block = jnp.concatenate(rows, 0).astype(bf16)
    for z in range(NZ):
        w_ref[z] = block


def spread(msg):
    return pl.pallas_call(
        spread_kernel,
        grid=(1,),
        in_specs=[pl.BlockSpec((NY, MSG - W0, HD), lambda i: (0, W0 // (MSG - W0), 0))],
        out_specs=pl.BlockSpec(memory_space=pltpu.VMEM),
        out_shape=jax.ShapeDtypeStruct((NZ, 2 * GRP * NY * ROWS, HD), bf16),
        name="spread",
    )(msg)


def relay_kernel(where_ref, key_ref, *out_refs):
    own_y = where_ref[2]
    for t, ref in enumerate(out_refs):
        rows = KEY_K + (own_y ^ t) * (GRP * RD)
        ref[0:KEY_K, :] = key_ref[0:KEY_K, :]
        ref[KEY_K:PASS_S, :] = key_ref[pl.ds(pl.multiple_of(rows, GRP * RD), GRP * RD), :]
        ref[PASS_S:PASS, :] = key_ref[KEY_S:KEY, :]


def relay(place, other):
    return pl.pallas_call(
        relay_kernel,
        in_specs=[
            pl.BlockSpec(memory_space=pltpu.SMEM),
            pl.BlockSpec(memory_space=pltpu.VMEM),
        ],
        out_shape=[jax.ShapeDtypeStruct((PASS, HD), bf16)] * NY,
        cost_estimate=waits_for_z,
        name="relay",
    )(place, other)


def main_kernel(
    where_ref, freq_ref, msg_ref, key0_ref, key1_ref, key2_ref, key3_ref, w_ref,
    lat_out_ref, dq_ref, kr_own_ref, kr_other_ref, dw_own_ref, dw_other_ref,
    lat_s, w_s, k_s, kt_s, q_s, qt_s, v_s, gt_s, pos_s, rope_s, cos_s, sin_s, dkv_s, dqt_s, dw_s,
):
    core = where_ref[0]
    own_y = where_ref[2]
    def take(read, lat0, rope0, pos0, tokens):
        for b in range(RANK // HD):
            lat_s[tokens, b * HD:(b + 1) * HD] = read(lat0 + b * TOK, TOK)
        rope_s[:, tokens] = read(rope0, GRP * RD).astype(f32)
        tail = read(pos0, 16).astype(f32)
        pos_s[0:1, tokens] = tail[0:1] * 64.0 + tail[1:2]

    for y in range(NY):
        take(
            lambda r, n, y=y: msg_ref[y, r:r + n, :], L0, K0, S0,
            slice(y * TOK, (y + 1) * TOK),
        )
    for t, ref in enumerate((key0_ref, key1_ref, key2_ref, key3_ref)):
        tokens = pl.ds(pl.multiple_of((NY + (own_y ^ t)) * TOK, TOK), TOK)
        take(lambda r, n, ref=ref: ref[r:r + n, :], 0, KEY_K, PASS_S, tokens)
    for z in range(NZ):
        for c in range(CORE):
            r = ((z // 2) * CORE + c) * 32 + (z % 2) * 16
            for kind in range(2 * GRP):
                w_s[r:r + 16, kind * HD:(kind + 1) * HD] = w_ref[c, z, kind * 16:(kind + 1) * 16, :]
    pos_row = pos_s[0:1, :]
    freq = freq_ref[...].astype(f32)
    heads = lax.broadcasted_iota(jnp.int32, freq.shape, 0)
    diagonal = lax.broadcasted_iota(jnp.int32, (HALF_RD, HALF_RD), 0) == lax.broadcasted_iota(
        jnp.int32, (HALF_RD, HALF_RD), 1
    )
    columns = []
    for g in range(GRP):
        row = jnp.sum(jnp.where(heads == own_y * GRP + g, freq, 0.0), 0, keepdims=True)
        columns.append(jnp.sum(jnp.where(diagonal, row, 0.0), 1, keepdims=True))
    inverse = jnp.exp(jnp.concatenate(columns, 0) * (-2.0 / HD * math.log(rope_base)))
    angles = inverse * pos_row
    cos_s[...] = jnp.cos(angles)
    sin_s[...] = jnp.sin(angles)
    pos_col = jnp.broadcast_to(pos_row, (8, SEQ)).T[:, 0:1]
    scale = HD ** -0.5
    kv = dot(lat_s[...], w_s[...])
    dkv_s[...] = jnp.zeros_like(dkv_s)

    for g in range(GRP):
        cos = cos_s[g * HALF_RD:(g + 1) * HALF_RD, :]
        sin = sin_s[g * HALF_RD:(g + 1) * HALF_RD, :]

        def rot(a, width):
            a, b = a[:HALF_RD], a[HALF_RD:RD]
            c, s = cos[:, :width], sin[:, :width]
            return jnp.concatenate([a * c - b * s, b * c + a * s], 0)

        def unrot(a, width):
            a, b = a[:HALF_RD], a[HALF_RD:RD]
            c, s = cos[:, :width], sin[:, :width]
            return jnp.concatenate([a * c + b * s, b * c - a * s], 0)

        kr = rot(rope_s[g * RD:(g + 1) * RD, :], SEQ)
        kr_pad = jnp.concatenate([kr, jnp.zeros((HD - RD, SEQ), f32)], 0)
        k = kv[:, g * HD:(g + 1) * HD] + kr_pad.T
        k_s[...] = k.astype(bf16)
        kt_s[...] = k.T.astype(bf16)
        v_s[...] = kv[:, (GRP + g) * HD:(GRP + g + 1) * HD].astype(bf16)
        for c in range(NY):
            cols = slice(c * TOK, (c + 1) * TOK)
            qt_s[:, cols] = msg_ref[c, Q0 + g * TOK:Q0 + (g + 1) * TOK, :].astype(f32).T
            gt_s[:, cols] = msg_ref[c, G0 + g * TOK:G0 + (g + 1) * TOK, :].astype(f32).T.astype(bf16)
        qt_s[0:RD, :] = rot(qt_s[0:RD, :], HALF)
        qt = qt_s[...]
        q_s[...] = qt.T.astype(bf16)

        for b in range(HALF // BLK):
            cols = slice(b * BLK, (b + 1) * BLK)
            st = dot(k_s[...], qt[:, cols].astype(bf16))
            visible = pos_col <= pos_row[:, cols]
            st = jnp.where(visible, st * (scale * log2_e), neg_large)
            top = jnp.max(st, 0, keepdims=True)
            e = jnp.exp2(st - top)
            dp = dot(v_s[...], gt_s[:, cols])
            total = jnp.sum(e, 0, keepdims=True)
            weighted = jnp.sum(e * dp, 0, keepdims=True)
            inv_total = 1.0 / total
            delta = weighted * inv_total
            probs = (e * inv_total).astype(bf16)
            ds = (scale * probs.astype(f32) * (dp - delta)).astype(bf16)
            dqt_s[:, cols] = dot(kt_s[...], ds)
            dkv_s[:, g * HD:(g + 1) * HD] += dot(ds, q_s[cols, :])
            grad = jnp.concatenate(
                [
                    msg_ref[c, G0 + g * TOK:G0 + (g + 1) * TOK, :]
                    for c in range(b * BLK // TOK, (b + 1) * BLK // TOK)
                ],
                0,
            )
            dkv_s[:, (GRP + g) * HD:(GRP + g + 1) * HD] += dot(probs, grad)

        dqt_s[0:RD, :] = unrot(dqt_s[0:RD, :], HALF)
        dq = dqt_s[...].T.astype(bf16)
        dkr = unrot(dkv_s[:, g * HD:(g + 1) * HD].T[0:RD, :], SEQ).astype(bf16)
        for c in range(NY):
            cols = slice(c * TOK, (c + 1) * TOK)
            dq_ref[c, g * TOK:(g + 1) * TOK, :] = dq[cols, :]
            kr_own_ref[c, g * RD:(g + 1) * RD, :] = dkr[:, cols]
            kr_other_ref[c, g * RD:(g + 1) * RD, :] = dkr[:, HALF + c * TOK:HALF + (c + 1) * TOK]

    dkv = dkv_s[...].astype(bf16)
    dlat = dot(dkv, w_s[...], ((1,), (1,))).astype(bf16)
    for z in range(2):
        for y in range(NY):
            c = z * NY + y
            for b in range(TEN):
                lat_out_ref[y * TEN + b, z * TOK:(z + 1) * TOK, :] = dlat[
                    c * TOK:(c + 1) * TOK, b * HD:(b + 1) * HD
                ]
    dw_s[...] = dot(lat_s[...], dkv, ((0,), (0,)))
    for z in range(NZ):
        base = (z // 2) * CORE * 32 + (z % 2) * 16
        own = pl.ds(pl.multiple_of(base + core * 32, 16), 16)
        other = pl.ds(pl.multiple_of(base + (1 - core) * 32, 16), 16)
        dw_own_ref[z] = dw_s[own, :].astype(bf16)
        dw_other_ref[z] = dw_s[other, :].astype(bf16)


def attention(place, freq, msg, keys, w):
    smem = pl.BlockSpec(memory_space=pltpu.SMEM)
    vmem = pl.BlockSpec(memory_space=pltpu.VMEM)
    return pl.pallas_call(
        main_kernel,
        in_specs=[smem] + [vmem] * 7,
        out_specs=[vmem] * 6,
        out_shape=[
            jax.ShapeDtypeStruct((NY * TEN, 2 * TOK, HD), bf16),
            jax.ShapeDtypeStruct((NY, GRP * TOK, HD), bf16),
            jax.ShapeDtypeStruct((NY, GRP * RD, TOK), bf16),
            jax.ShapeDtypeStruct((NY, GRP * RD, TOK), bf16),
            jax.ShapeDtypeStruct((NZ, NY * ROWS, 2 * GRP * HD), bf16),
            jax.ShapeDtypeStruct((NZ, NY * ROWS, 2 * GRP * HD), bf16),
        ],
        scratch_shapes=[
            pltpu.VMEM((SEQ, RANK), bf16),
            pltpu.VMEM((RANK, 2 * GRP * HD), bf16),
            pltpu.VMEM((SEQ, HD), bf16),
            pltpu.VMEM((HD, SEQ), bf16),
            pltpu.VMEM((HALF, HD), bf16),
            pltpu.VMEM((HD, HALF), f32),
            pltpu.VMEM((SEQ, HD), bf16),
            pltpu.VMEM((HD, HALF), bf16),
            pltpu.VMEM((8, SEQ), f32),
            pltpu.VMEM((GRP * RD, SEQ), f32),
            pltpu.VMEM((GRP * HALF_RD, SEQ), f32),
            pltpu.VMEM((GRP * HALF_RD, SEQ), f32),
            pltpu.VMEM((SEQ, 2 * GRP * HD), f32),
            pltpu.VMEM((HD, HALF), f32),
            pltpu.VMEM((RANK, 2 * GRP * HD), f32),
        ],
        compiler_params=pltpu.CompilerParams(vmem_limit_bytes=56 * 1024 * 1024),
        name="attention_backward",
    )(place, freq, msg, *keys, w)


def fold_kernel(parts_ref, dw0_ref, dw1_ref, kr_ref, own_ref, other_ref, dw_ref):
    both = jnp.sum(parts_ref[...].astype(f32), 0)
    own_ref[...] = both[0:TOK]
    other_ref[0:TOK, :] = both[TOK:].astype(bf16)
    for y in range(NY):
        other_ref[TOK + y * GRP * RD:TOK + (y + 1) * GRP * RD, :] = kr_ref[y]
    dw_ref[...] = (dw0_ref[...].astype(f32) + dw1_ref[...].astype(f32)).astype(bf16)


def fold(*parts):
    return pl.pallas_call(
        fold_kernel,
        out_shape=[
            jax.ShapeDtypeStruct((TOK, HD), f32),
            jax.ShapeDtypeStruct((TOK + NY * GRP * RD, HD), bf16),
            jax.ShapeDtypeStruct((NZ, NY * ROWS, 2 * GRP * HD), bf16),
        ],
        name="fold",
    )(*parts)


def merge_kernel(own_ref, kr_ref, other_ref, quarter_ref, out_ref):
    quarter_ref[...] = (own_ref[...] + other_ref[0:TOK, :].astype(f32)).astype(bf16)
    for y in range(NY):
        kr = other_ref[TOK + y * GRP * RD:TOK + (y + 1) * GRP * RD, :]
        out_ref[y] = (kr_ref[y].astype(f32) + kr.astype(f32)).astype(bf16)


def merge(*parts):
    return pl.pallas_call(
        merge_kernel,
        out_shape=[
            jax.ShapeDtypeStruct((TOK, HD), bf16),
            jax.ShapeDtypeStruct((NY, GRP * RD, TOK), bf16),
        ],
        cost_estimate=waits_for_z,
        name="merge",
    )(*parts)


def combine_kernel(
    where_ref, dq_ref, kr_ref, dw_ref, q0_ref, q1_ref, q2_ref, q3_ref, out_ref, lat_ref
):
    x = where_ref[1]
    for t, ref in enumerate((q0_ref, q1_ref, q2_ref, q3_ref)):
        lat_ref[:, pl.ds(pl.multiple_of((x ^ t) * HD, HD), HD)] = ref[...]
    dw = jnp.sum(dw_ref[...].astype(f32), 0)
    for y in range(NY):
        out_ref[y, 0:BK0, :] = dq_ref[y]
        out_ref[y, BK0:BW0, :] = kr_ref[y]
        part = dw[y * ROWS:(y + 1) * ROWS, :]
        out_ref[y, BW0:BACK, :] = jnp.concatenate(
            [part[:, c * HD:(c + 1) * HD] for c in range(2 * GRP)], 0
        ).astype(bf16)


def combine(place, *parts):
    vmem = pl.BlockSpec(memory_space=pltpu.VMEM)
    return pl.pallas_call(
        combine_kernel,
        in_specs=[pl.BlockSpec(memory_space=pltpu.SMEM)] + [vmem] * (3 + TEN),
        out_shape=[
            jax.ShapeDtypeStruct((NY, BACK, HD), bf16),
            jax.ShapeDtypeStruct((TOK, RANK), bf16),
        ],
        name="combine",
    )(place, *parts)


def unpack_kernel(msg_ref, q_ref, kr_ref, wk_ref, wv_ref):
    ropes = []
    wk = []
    wv = []
    for y in range(NY):
        for g in range(GRP):
            h = y * GRP + g
            q_ref[:, h * HD:(h + 1) * HD] = msg_ref[y, g * TOK:(g + 1) * TOK, :]
        ropes.append(msg_ref[y, BK0:BW0, :].astype(f32))
        tail = msg_ref[y, BW0:BACK, :].astype(f32)
        for g in range(GRP):
            wk.append(tail[g * ROWS:(g + 1) * ROWS, RD:])
            wv.append(tail[(GRP + g) * ROWS:(GRP + g + 1) * ROWS])
    kr_ref[...] = jnp.concatenate(ropes, 0).T.astype(bf16)
    wk_ref[...] = jnp.concatenate(wk, 1).astype(bf16)
    wv_ref[...] = jnp.concatenate(wv, 1).astype(bf16)


def unpack(msg):
    return pl.pallas_call(
        unpack_kernel,
        out_shape=[
            jax.ShapeDtypeStruct((TOK, NY * GRP * HD), bf16),
            jax.ShapeDtypeStruct((TOK, NY * GRP * RD), bf16),
            jax.ShapeDtypeStruct((ROWS, NY * GRP * NOPE), bf16),
            jax.ShapeDtypeStruct((ROWS, NY * GRP * HD), bf16),
        ],
        name="unpack",
    )(msg)


def swap(array, axis, size, flip):
    return lax.ppermute(array, axis, [(i, i ^ flip) for i in range(size)])


def body(latent, key_rope, query, out_grad, positions, freq_index, up_key, up_value):
    place = jnp.stack([lax.axis_index(a).astype(jnp.int32) for a in ("core", "x", "y", "zh")])

    msg, own = pack(query[0], out_grad[0], key_rope[0], latent[0], up_key, up_value, positions)
    other = swap(own, "zh", 2, 1)
    msg = lax.all_to_all(msg, "y", 0, 0)
    w = lax.all_to_all(spread(msg), ("zl", "zh"), 0, 0)
    keys = relay(place, other)
    keys = [keys[0]] + [swap(keys[t], "y", NY, t) for t in range(1, NY)]
    w = lax.all_gather(w, "core", axis=0)

    parts, dq, kr_own, kr_other, dw_own, dw_other = attention(place, freq_index, msg, keys, w)

    dw_other = swap(dw_other, "core", 2, 1)
    parts = lax.all_to_all(parts, ("y", "x"), 0, 0)
    lat_own, other, dw = fold(parts, dw_own, dw_other, kr_other)
    other = swap(other, "zh", 2, 1)
    dw = lax.all_to_all(dw, ("zl", "zh"), 0, 0)
    quarter, kr = merge(lat_own, kr_own, other)
    quarters = [quarter] + [swap(quarter, "x", TEN, t) for t in range(1, TEN)]
    back, latent_grad = combine(place, dq, kr, dw, *quarters)
    back = lax.all_to_all(back, "y", 0, 0)
    query_grad, key_rope_grad, up_key_grad, up_value_grad = unpack(back)
    return (query_grad[None], key_rope_grad[None], latent_grad[None], up_key_grad, up_value_grad)


def solution(mesh):
    split = Mesh(mesh.devices.reshape(ZL, CORE, 2, NY, TEN), ("zl", "core", "zh", "y", "x"))
    dp, context, tensor = ("zl", "core"), ("zh", "y"), "x"
    return jax.shard_map(
        body,
        mesh=split,
        in_specs=(
            P(dp, context, None),
            P(dp, context, tensor),
            P(dp, context, tensor),
            P(dp, context, tensor),
            P(dp, context),
            P(tensor, None),
            P(dp + context, tensor),
            P(dp + context, tensor),
        ),
        out_specs=(
            P(dp, context, tensor),
            P(dp, context, tensor),
            P(dp, context, None),
            P(dp + context, tensor),
            P(dp + context, tensor),
        ),
        check_vma=False,
    )
```

```python
import math

import jax
import jax.numpy as jnp
from jax import lax
from jax.experimental import pallas as pl
from jax.experimental.pallas import tpu as pltpu
from jax.sharding import Mesh, PartitionSpec as P

rope_base = 500000.0
neg_large = -1e30
log2_e = 1.4426950408889634

NY = 4
GRP = 2
TOK = 128
HALF = NY * TOK
SEQ = 2 * HALF
HD = 128
RD = 32
HALF_RD = 16
NOPE = 96
RANK = 512
ROWS = 4
ZL = 8
CORE = 2
NZ = 2 * ZL
TEN = 4
Q0, G0, L0, K0, S0, W0, MSG = 0, 256, 512, 1024, 1088, 1104, 1120
KEY_K, KEY_S, KEY = 512, 768, 784
PASS_S, PASS = 576, 592
BK0, BW0, BACK = 256, 320, 336
BLK = 512

waits_for_z = pl.CostEstimate(flops=50_000_000_000, transcendentals=0, bytes_accessed=150_000_000)
f32 = jnp.float32
bf16 = jnp.bfloat16


def dot(a, b, dims=((1,), (0,))):
    return lax.dot_general(a, b, (dims, ((), ())), preferred_element_type=f32)


def pack_kernel(q_ref, g_ref, kr_ref, lat_ref, wk_ref, wv_ref, pos_ref, out_ref, key_ref):
    rope_t = kr_ref[...].astype(f32).T.astype(bf16)
    pos = pos_ref[...]
    places = jnp.concatenate(
        [(pos >> 6).astype(f32), (pos & 63).astype(f32), jnp.zeros((14, TOK), f32)], 0
    ).astype(bf16)
    for b in range(RANK // HD):
        key_ref[b * TOK:(b + 1) * TOK, :] = lat_ref[:, b * HD:(b + 1) * HD]
    key_ref[KEY_K:KEY_S, :] = rope_t
    key_ref[KEY_S:KEY, :] = places
    wk = wk_ref[...].astype(f32)
    wv = wv_ref[...].astype(f32)
    for y in range(NY):
        parts_k = []
        parts_v = []
        for g in range(GRP):
            h = y * GRP + g
            cols = slice(h * HD, (h + 1) * HD)
            out_ref[y, Q0 + g * TOK:Q0 + (g + 1) * TOK, :] = q_ref[:, cols]
            out_ref[y, G0 + g * TOK:G0 + (g + 1) * TOK, :] = g_ref[:, cols]
            parts_v.append(wv[:, cols])
            parts_k.append(
                jnp.concatenate([jnp.zeros((ROWS, RD), f32), wk[:, h * NOPE:(h + 1) * NOPE]], 1)
            )
        for b in range(RANK // HD):
            out_ref[y, L0 + b * TOK:L0 + (b + 1) * TOK, :] = lat_ref[:, b * HD:(b + 1) * HD]
        out_ref[y, K0:S0, :] = rope_t[y * GRP * RD:(y + 1) * GRP * RD, :]
        out_ref[y, S0:W0, :] = places
        out_ref[y, W0:MSG, :] = jnp.concatenate(parts_k + parts_v, 0).astype(bf16)


def pack(*parts):
    return pl.pallas_call(
        pack_kernel,
        out_shape=[
            jax.ShapeDtypeStruct((NY, MSG, HD), bf16),
            jax.ShapeDtypeStruct((KEY, HD), bf16),
        ],
        name="pack",
    )(*parts)


def spread_kernel(msg_ref, w_ref):
    tails = [msg_ref[y].astype(f32) for y in range(NY)]
    rows = [tails[y][c * ROWS:(c + 1) * ROWS] for c in range(2 * GRP) for y in range(NY)]
    block = jnp.concatenate(rows, 0).astype(bf16)
    for z in range(NZ):
        w_ref[z] = block


def spread(msg):
    return pl.pallas_call(
        spread_kernel,
        grid=(1,),
        in_specs=[pl.BlockSpec((NY, MSG - W0, HD), lambda i: (0, W0 // (MSG - W0), 0))],
        out_specs=pl.BlockSpec(memory_space=pltpu.VMEM),
        out_shape=jax.ShapeDtypeStruct((NZ, 2 * GRP * NY * ROWS, HD), bf16),
        name="spread",
    )(msg)


def relay_kernel(where_ref, key_ref, *out_refs):
    own_y = where_ref[2]
    for t, ref in enumerate(out_refs):
        rows = KEY_K + (own_y ^ t) * (GRP * RD)
        ref[0:KEY_K, :] = key_ref[0:KEY_K, :]
        ref[KEY_K:PASS_S, :] = key_ref[pl.ds(pl.multiple_of(rows, GRP * RD), GRP * RD), :]
        ref[PASS_S:PASS, :] = key_ref[KEY_S:KEY, :]


def relay(place, other):
    return pl.pallas_call(
        relay_kernel,
        in_specs=[
            pl.BlockSpec(memory_space=pltpu.SMEM),
            pl.BlockSpec(memory_space=pltpu.VMEM),
        ],
        out_shape=[jax.ShapeDtypeStruct((PASS, HD), bf16)] * NY,
        cost_estimate=waits_for_z,
        name="relay",
    )(place, other)


def main_kernel(
    where_ref, freq_ref, msg_ref, key0_ref, key1_ref, key2_ref, key3_ref, w_ref,
    lat_out_ref, dq_ref, kr_own_ref, kr_other_ref, dw_own_ref, dw_other_ref,
    lat_s, w_s, k_s, kt_s, q_s, qt_s, v_s, gt_s, pos_s, rope_s, cos_s, sin_s, dkv_s, dqt_s, dw_s,
):
    core = where_ref[0]
    own_y = where_ref[2]
    def take(read, lat0, rope0, pos0, tokens):
        for b in range(RANK // HD):
            lat_s[tokens, b * HD:(b + 1) * HD] = read(lat0 + b * TOK, TOK)
        rope_s[:, tokens] = read(rope0, GRP * RD).astype(f32)
        tail = read(pos0, 16).astype(f32)
        pos_s[0:1, tokens] = tail[0:1] * 64.0 + tail[1:2]

    for y in range(NY):
        take(
            lambda r, n, y=y: msg_ref[y, r:r + n, :], L0, K0, S0,
            slice(y * TOK, (y + 1) * TOK),
        )
    for t, ref in enumerate((key0_ref, key1_ref, key2_ref, key3_ref)):
        tokens = pl.ds(pl.multiple_of((NY + (own_y ^ t)) * TOK, TOK), TOK)
        take(lambda r, n, ref=ref: ref[r:r + n, :], 0, KEY_K, PASS_S, tokens)
    for z in range(NZ):
        for c in range(CORE):
            r = ((z // 2) * CORE + c) * 32 + (z % 2) * 16
            for kind in range(2 * GRP):
                w_s[r:r + 16, kind * HD:(kind + 1) * HD] = w_ref[c, z, kind * 16:(kind + 1) * 16, :]
    pos_row = pos_s[0:1, :]
    freq = freq_ref[...].astype(f32)
    heads = lax.broadcasted_iota(jnp.int32, freq.shape, 0)
    diagonal = lax.broadcasted_iota(jnp.int32, (HALF_RD, HALF_RD), 0) == lax.broadcasted_iota(
        jnp.int32, (HALF_RD, HALF_RD), 1
    )
    columns = []
    for g in range(GRP):
        row = jnp.sum(jnp.where(heads == own_y * GRP + g, freq, 0.0), 0, keepdims=True)
        columns.append(jnp.sum(jnp.where(diagonal, row, 0.0), 1, keepdims=True))
    inverse = jnp.exp(jnp.concatenate(columns, 0) * (-2.0 / HD * math.log(rope_base)))
    angles = inverse * pos_row
    cos_s[...] = jnp.cos(angles)
    sin_s[...] = jnp.sin(angles)
    pos_col = jnp.broadcast_to(pos_row, (8, SEQ)).T[:, 0:1]
    scale = HD ** -0.5
    kv = dot(lat_s[...], w_s[...])
    dkv_s[...] = jnp.zeros_like(dkv_s)

    for g in range(GRP):
        cos = cos_s[g * HALF_RD:(g + 1) * HALF_RD, :]
        sin = sin_s[g * HALF_RD:(g + 1) * HALF_RD, :]

        def rot(a, width):
            a, b = a[:HALF_RD], a[HALF_RD:RD]
            c, s = cos[:, :width], sin[:, :width]
            return jnp.concatenate([a * c - b * s, b * c + a * s], 0)

        def unrot(a, width):
            a, b = a[:HALF_RD], a[HALF_RD:RD]
            c, s = cos[:, :width], sin[:, :width]
            return jnp.concatenate([a * c + b * s, b * c - a * s], 0)

        kr = rot(rope_s[g * RD:(g + 1) * RD, :], SEQ)
        kr_pad = jnp.concatenate([kr, jnp.zeros((HD - RD, SEQ), f32)], 0)
        k = kv[:, g * HD:(g + 1) * HD] + kr_pad.T
        k_s[...] = k.astype(bf16)
        kt_s[...] = k.T.astype(bf16)
        v_s[...] = kv[:, (GRP + g) * HD:(GRP + g + 1) * HD].astype(bf16)
        for c in range(NY):
            cols = slice(c * TOK, (c + 1) * TOK)
            qt_s[:, cols] = msg_ref[c, Q0 + g * TOK:Q0 + (g + 1) * TOK, :].astype(f32).T
            gt_s[:, cols] = msg_ref[c, G0 + g * TOK:G0 + (g + 1) * TOK, :].astype(f32).T.astype(bf16)
        qt_s[0:RD, :] = rot(qt_s[0:RD, :], HALF)
        qt = qt_s[...]
        q_s[...] = qt.T.astype(bf16)

        for b in range(HALF // BLK):
            cols = slice(b * BLK, (b + 1) * BLK)
            st = dot(k_s[...], qt[:, cols].astype(bf16))
            visible = pos_col <= pos_row[:, cols]
            st = jnp.where(visible, st * (scale * log2_e), neg_large)
            top = jnp.max(st, 0, keepdims=True)
            e = jnp.exp2(st - top)
            dp = dot(v_s[...], gt_s[:, cols])
            total = jnp.sum(e, 0, keepdims=True)
            weighted = jnp.sum(e * dp, 0, keepdims=True)
            inv_total = 1.0 / total
            delta = weighted * inv_total
            probs = (e * inv_total).astype(bf16)
            ds = (scale * probs.astype(f32) * (dp - delta)).astype(bf16)
            dqt_s[:, cols] = dot(kt_s[...], ds)
            dkv_s[:, g * HD:(g + 1) * HD] += dot(ds, q_s[cols, :])
            grad = jnp.concatenate(
                [
                    msg_ref[c, G0 + g * TOK:G0 + (g + 1) * TOK, :]
                    for c in range(b * BLK // TOK, (b + 1) * BLK // TOK)
                ],
                0,
            )
            dkv_s[:, (GRP + g) * HD:(GRP + g + 1) * HD] += dot(probs, grad)

        dqt_s[0:RD, :] = unrot(dqt_s[0:RD, :], HALF)
        dq = dqt_s[...].T.astype(bf16)
        dkr = unrot(dkv_s[:, g * HD:(g + 1) * HD].T[0:RD, :], SEQ).astype(bf16)
        for c in range(NY):
            cols = slice(c * TOK, (c + 1) * TOK)
            dq_ref[c, g * TOK:(g + 1) * TOK, :] = dq[cols, :]
            kr_own_ref[c, g * RD:(g + 1) * RD, :] = dkr[:, cols]
            kr_other_ref[c, g * RD:(g + 1) * RD, :] = dkr[:, HALF + c * TOK:HALF + (c + 1) * TOK]

    dkv = dkv_s[...].astype(bf16)
    dlat = dot(dkv, w_s[...], ((1,), (1,))).astype(bf16)
    for z in range(2):
        for y in range(NY):
            c = z * NY + y
            for b in range(TEN):
                lat_out_ref[y * TEN + b, z * TOK:(z + 1) * TOK, :] = dlat[
                    c * TOK:(c + 1) * TOK, b * HD:(b + 1) * HD
                ]
    dw_s[...] = dot(lat_s[...], dkv, ((0,), (0,)))
    for z in range(NZ):
        base = (z // 2) * CORE * 32 + (z % 2) * 16
        own = pl.ds(pl.multiple_of(base + core * 32, 16), 16)
        other = pl.ds(pl.multiple_of(base + (1 - core) * 32, 16), 16)
        dw_own_ref[z] = dw_s[own, :].astype(bf16)
        dw_other_ref[z] = dw_s[other, :].astype(bf16)


def attention(place, freq, msg, keys, w):
    smem = pl.BlockSpec(memory_space=pltpu.SMEM)
    vmem = pl.BlockSpec(memory_space=pltpu.VMEM)
    return pl.pallas_call(
        main_kernel,
        in_specs=[smem] + [vmem] * 7,
        out_specs=[vmem] * 6,
        out_shape=[
            jax.ShapeDtypeStruct((NY * TEN, 2 * TOK, HD), bf16),
            jax.ShapeDtypeStruct((NY, GRP * TOK, HD), bf16),
            jax.ShapeDtypeStruct((NY, GRP * RD, TOK), bf16),
            jax.ShapeDtypeStruct((NY, GRP * RD, TOK), bf16),
            jax.ShapeDtypeStruct((NZ, NY * ROWS, 2 * GRP * HD), bf16),
            jax.ShapeDtypeStruct((NZ, NY * ROWS, 2 * GRP * HD), bf16),
        ],
        scratch_shapes=[
            pltpu.VMEM((SEQ, RANK), bf16),
            pltpu.VMEM((RANK, 2 * GRP * HD), bf16),
            pltpu.VMEM((SEQ, HD), bf16),
            pltpu.VMEM((HD, SEQ), bf16),
            pltpu.VMEM((HALF, HD), bf16),
            pltpu.VMEM((HD, HALF), f32),
            pltpu.VMEM((SEQ, HD), bf16),
            pltpu.VMEM((HD, HALF), bf16),
            pltpu.VMEM((8, SEQ), f32),
            pltpu.VMEM((GRP * RD, SEQ), f32),
            pltpu.VMEM((GRP * HALF_RD, SEQ), f32),
            pltpu.VMEM((GRP * HALF_RD, SEQ), f32),
            pltpu.VMEM((SEQ, 2 * GRP * HD), f32),
            pltpu.VMEM((HD, HALF), f32),
            pltpu.VMEM((RANK, 2 * GRP * HD), f32),
        ],
        compiler_params=pltpu.CompilerParams(vmem_limit_bytes=56 * 1024 * 1024),
        name="attention_backward",
    )(place, freq, msg, *keys, w)


def fold_kernel(parts_ref, dw0_ref, dw1_ref, own_ref, other_ref, dw_ref):
    both = jnp.sum(parts_ref[...].astype(f32), 0)
    own_ref[...] = both[0:TOK]
    other_ref[...] = both[TOK:].astype(bf16)
    dw_ref[...] = (dw0_ref[...].astype(f32) + dw1_ref[...].astype(f32)).astype(bf16)


def fold(*parts):
    return pl.pallas_call(
        fold_kernel,
        out_shape=[
            jax.ShapeDtypeStruct((TOK, HD), f32),
            jax.ShapeDtypeStruct((TOK, HD), bf16),
            jax.ShapeDtypeStruct((NZ, NY * ROWS, 2 * GRP * HD), bf16),
        ],
        name="fold",
    )(*parts)


def merge_kernel(own_ref, other_ref, kr0_ref, kr1_ref, quarter_ref, kr_ref):
    quarter_ref[...] = (own_ref[...] + other_ref[...].astype(f32)).astype(bf16)
    kr_ref[...] = (kr0_ref[...].astype(f32) + kr1_ref[...].astype(f32)).astype(bf16)


def merge(*parts):
    return pl.pallas_call(
        merge_kernel,
        out_shape=[
            jax.ShapeDtypeStruct((TOK, HD), bf16),
            jax.ShapeDtypeStruct((NY, GRP * RD, TOK), bf16),
        ],
        cost_estimate=waits_for_z,
        name="merge",
    )(*parts)


def combine_kernel(
    where_ref, dq_ref, kr_ref, dw_ref, q0_ref, q1_ref, pair_ref, out_ref, lat_ref
):
    x = where_ref[1]
    for t, ref in enumerate((q0_ref, q1_ref)):
        lat_ref[:, pl.ds(pl.multiple_of((x ^ t) * HD, HD), HD)] = ref[...]
    for t in range(2):
        cols = pl.ds(pl.multiple_of((x ^ 3 ^ t) * HD, HD), HD)
        lat_ref[:, cols] = pair_ref[t * TOK:(t + 1) * TOK, :]
    dw = jnp.sum(dw_ref[...].astype(f32), 0)
    for y in range(NY):
        out_ref[y, 0:BK0, :] = dq_ref[y]
        out_ref[y, BK0:BW0, :] = kr_ref[y]
        part = dw[y * ROWS:(y + 1) * ROWS, :]
        out_ref[y, BW0:BACK, :] = jnp.concatenate(
            [part[:, c * HD:(c + 1) * HD] for c in range(2 * GRP)], 0
        ).astype(bf16)


def combine(place, *parts):
    vmem = pl.BlockSpec(memory_space=pltpu.VMEM)
    return pl.pallas_call(
        combine_kernel,
        in_specs=[pl.BlockSpec(memory_space=pltpu.SMEM)] + [vmem] * 6,
        out_shape=[
            jax.ShapeDtypeStruct((NY, BACK, HD), bf16),
            jax.ShapeDtypeStruct((TOK, RANK), bf16),
        ],
        name="combine",
    )(place, *parts)


def unpack_kernel(msg_ref, q_ref, kr_ref, wk_ref, wv_ref):
    ropes = []
    wk = []
    wv = []
    for y in range(NY):
        for g in range(GRP):
            h = y * GRP + g
            q_ref[:, h * HD:(h + 1) * HD] = msg_ref[y, g * TOK:(g + 1) * TOK, :]
        ropes.append(msg_ref[y, BK0:BW0, :].astype(f32))
        tail = msg_ref[y, BW0:BACK, :].astype(f32)
        for g in range(GRP):
            wk.append(tail[g * ROWS:(g + 1) * ROWS, RD:])
            wv.append(tail[(GRP + g) * ROWS:(GRP + g + 1) * ROWS])
    kr_ref[...] = jnp.concatenate(ropes, 0).T.astype(bf16)
    wk_ref[...] = jnp.concatenate(wk, 1).astype(bf16)
    wv_ref[...] = jnp.concatenate(wv, 1).astype(bf16)


def unpack(msg):
    return pl.pallas_call(
        unpack_kernel,
        out_shape=[
            jax.ShapeDtypeStruct((TOK, NY * GRP * HD), bf16),
            jax.ShapeDtypeStruct((TOK, NY * GRP * RD), bf16),
            jax.ShapeDtypeStruct((ROWS, NY * GRP * NOPE), bf16),
            jax.ShapeDtypeStruct((ROWS, NY * GRP * HD), bf16),
        ],
        name="unpack",
    )(msg)


def swap(array, axis, size, flip):
    return lax.ppermute(array, axis, [(i, i ^ flip) for i in range(size)])


def body(latent, key_rope, query, out_grad, positions, freq_index, up_key, up_value):
    place = jnp.stack([lax.axis_index(a).astype(jnp.int32) for a in ("core", "x", "y", "zh")])

    msg, own = pack(query[0], out_grad[0], key_rope[0], latent[0], up_key, up_value, positions)
    other = swap(own, "zh", 2, 1)
    msg = lax.all_to_all(msg, "y", 0, 0)
    w = lax.all_to_all(spread(msg), ("zl", "zh"), 0, 0)
    keys = relay(place, other)
    keys = [keys[0]] + [swap(keys[t], "y", NY, t) for t in range(1, NY)]
    w = lax.all_gather(w, "core", axis=0)

    parts, dq, kr_own, kr_other, dw_own, dw_other = attention(place, freq_index, msg, keys, w)

    dw_other = swap(dw_other, "core", 2, 1)
    parts = lax.all_to_all(parts, ("y", "x"), 0, 0)
    lat_own, other, dw = fold(parts, dw_own, dw_other)
    other = swap(other, "zh", 2, 1)
    kr_other = swap(kr_other, "zh", 2, 1)
    dw = lax.all_to_all(dw, ("zl", "zh"), 0, 0)
    quarter, kr = merge(lat_own, other, kr_own, kr_other)
    next_quarter = swap(quarter, "x", TEN, 1)
    pair = swap(jnp.concatenate([quarter, next_quarter], 0), "x", TEN, 3)
    back, latent_grad = combine(place, dq, kr, dw, quarter, next_quarter, pair)
    back = lax.all_to_all(back, "y", 0, 0)
    query_grad, key_rope_grad, up_key_grad, up_value_grad = unpack(back)
    return (query_grad[None], key_rope_grad[None], latent_grad[None], up_key_grad, up_value_grad)


def solution(mesh):
    split = Mesh(mesh.devices.reshape(ZL, CORE, 2, NY, TEN), ("zl", "core", "zh", "y", "x"))
    dp, context, tensor = ("zl", "core"), ("zh", "y"), "x"
    return jax.shard_map(
        body,
        mesh=split,
        in_specs=(
            P(dp, context, None),
            P(dp, context, tensor),
            P(dp, context, tensor),
            P(dp, context, tensor),
            P(dp, context),
            P(tensor, None),
            P(dp + context, tensor),
            P(dp + context, tensor),
        ),
        out_specs=(
            P(dp, context, tensor),
            P(dp, context, tensor),
            P(dp, context, None),
            P(dp + context, tensor),
            P(dp + context, tensor),
        ),
        check_vma=False,
    )
```

```python
import math

import jax
import jax.numpy as jnp
from jax import lax
from jax.experimental import pallas as pl
from jax.experimental.pallas import tpu as pltpu
from jax.sharding import Mesh, PartitionSpec as P

rope_base = 500000.0
neg_large = -1e30
log2_e = 1.4426950408889634

NY = 4
GRP = 2
TOK = 128
HALF = NY * TOK
SEQ = 2 * HALF
HD = 128
RD = 32
HALF_RD = 16
NOPE = 96
RANK = 512
ROWS = 4
ZL = 8
CORE = 2
NZ = 2 * ZL
TEN = 4
Q0, G0, L0, K0, S0, W0, MSG = 0, 256, 512, 1024, 1088, 1104, 1120
KEY_K, KEY_S, KEY = 512, 768, 784
PASS_S, PASS = 576, 592
BK0, BW0, BACK = 256, 320, 336
BLK = 512

waits_for_z = pl.CostEstimate(flops=50_000_000_000, transcendentals=0, bytes_accessed=150_000_000)
f32 = jnp.float32
bf16 = jnp.bfloat16


def dot(a, b, dims=((1,), (0,))):
    return lax.dot_general(a, b, (dims, ((), ())), preferred_element_type=f32)


def pack_kernel(q_ref, g_ref, kr_ref, lat_ref, wk_ref, wv_ref, pos_ref, out_ref, key_ref):
    rope_t = kr_ref[...].astype(f32).T.astype(bf16)
    pos = pos_ref[...]
    places = jnp.concatenate(
        [(pos >> 6).astype(f32), (pos & 63).astype(f32), jnp.zeros((14, TOK), f32)], 0
    ).astype(bf16)
    for b in range(RANK // HD):
        key_ref[b * TOK:(b + 1) * TOK, :] = lat_ref[:, b * HD:(b + 1) * HD]
    key_ref[KEY_K:KEY_S, :] = rope_t
    key_ref[KEY_S:KEY, :] = places
    wk = wk_ref[...].astype(f32)
    wv = wv_ref[...].astype(f32)
    for y in range(NY):
        parts_k = []
        parts_v = []
        for g in range(GRP):
            h = y * GRP + g
            cols = slice(h * HD, (h + 1) * HD)
            out_ref[y, Q0 + g * TOK:Q0 + (g + 1) * TOK, :] = q_ref[:, cols]
            out_ref[y, G0 + g * TOK:G0 + (g + 1) * TOK, :] = g_ref[:, cols]
            parts_v.append(wv[:, cols])
            parts_k.append(
                jnp.concatenate([jnp.zeros((ROWS, RD), f32), wk[:, h * NOPE:(h + 1) * NOPE]], 1)
            )
        for b in range(RANK // HD):
            out_ref[y, L0 + b * TOK:L0 + (b + 1) * TOK, :] = lat_ref[:, b * HD:(b + 1) * HD]
        out_ref[y, K0:S0, :] = rope_t[y * GRP * RD:(y + 1) * GRP * RD, :]
        out_ref[y, S0:W0, :] = places
        out_ref[y, W0:MSG, :] = jnp.concatenate(parts_k + parts_v, 0).astype(bf16)


def pack(*parts):
    return pl.pallas_call(
        pack_kernel,
        out_shape=[
            jax.ShapeDtypeStruct((NY, MSG, HD), bf16),
            jax.ShapeDtypeStruct((KEY, HD), bf16),
        ],
        name="pack",
    )(*parts)


def relay_kernel(where_ref, key_ref, *out_refs):
    own_y = where_ref[2]
    for t, ref in enumerate(out_refs):
        rows = KEY_K + (own_y ^ t) * (GRP * RD)
        ref[0:KEY_K, :] = key_ref[0:KEY_K, :]
        ref[KEY_K:PASS_S, :] = key_ref[pl.ds(pl.multiple_of(rows, GRP * RD), GRP * RD), :]
        ref[PASS_S:PASS, :] = key_ref[KEY_S:KEY, :]


def relay(place, other):
    return pl.pallas_call(
        relay_kernel,
        in_specs=[
            pl.BlockSpec(memory_space=pltpu.SMEM),
            pl.BlockSpec(memory_space=pltpu.VMEM),
        ],
        out_shape=[jax.ShapeDtypeStruct((PASS, HD), bf16)] * NY,
        cost_estimate=waits_for_z,
        name="relay",
    )(place, other)


def main_kernel(
    where_ref, freq_ref, msg_ref, key0_ref, key1_ref, key2_ref, key3_ref, w_ref,
    lat_out_ref, dq_ref, kr_own_ref, kr_other_ref, dw_own_ref, dw_other_ref,
    lat_s, w_s, k_s, kt_s, q_s, qt_s, v_s, gt_s, pos_s, rope_s, cos_s, sin_s, dkv_s, dqt_s, dw_s,
):
    core = where_ref[0]
    own_y = where_ref[2]
    def take(read, lat0, rope0, pos0, tokens):
        for b in range(RANK // HD):
            lat_s[tokens, b * HD:(b + 1) * HD] = read(lat0 + b * TOK, TOK)
        rope_s[:, tokens] = read(rope0, GRP * RD).astype(f32)
        tail = read(pos0, 16).astype(f32)
        pos_s[0:1, tokens] = tail[0:1] * 64.0 + tail[1:2]

    for y in range(NY):
        take(
            lambda r, n, y=y: msg_ref[y, r:r + n, :], L0, K0, S0,
            slice(y * TOK, (y + 1) * TOK),
        )
    for t, ref in enumerate((key0_ref, key1_ref, key2_ref, key3_ref)):
        tokens = pl.ds(pl.multiple_of((NY + (own_y ^ t)) * TOK, TOK), TOK)
        take(lambda r, n, ref=ref: ref[r:r + n, :], 0, KEY_K, PASS_S, tokens)
    for z in range(NZ):
        for c in range(CORE):
            r = ((z // 2) * CORE + c) * 32 + (z % 2) * 16
            for kind in range(2 * GRP):
                w_s[r:r + 16, kind * HD:(kind + 1) * HD] = w_ref[c, z, kind * 16:(kind + 1) * 16, :]
    pos_row = pos_s[0:1, :]
    freq = freq_ref[...].astype(f32)
    heads = lax.broadcasted_iota(jnp.int32, freq.shape, 0)
    diagonal = lax.broadcasted_iota(jnp.int32, (HALF_RD, HALF_RD), 0) == lax.broadcasted_iota(
        jnp.int32, (HALF_RD, HALF_RD), 1
    )
    columns = []
    for g in range(GRP):
        row = jnp.sum(jnp.where(heads == own_y * GRP + g, freq, 0.0), 0, keepdims=True)
        columns.append(jnp.sum(jnp.where(diagonal, row, 0.0), 1, keepdims=True))
    inverse = jnp.exp(jnp.concatenate(columns, 0) * (-2.0 / HD * math.log(rope_base)))
    angles = inverse * pos_row
    cos_s[...] = jnp.cos(angles)
    sin_s[...] = jnp.sin(angles)
    pos_col = jnp.broadcast_to(pos_row, (8, SEQ)).T[:, 0:1]
    scale = HD ** -0.5
    kv = dot(lat_s[...], w_s[...])
    dkv_s[...] = jnp.zeros_like(dkv_s)

    for g in range(GRP):
        cos = cos_s[g * HALF_RD:(g + 1) * HALF_RD, :]
        sin = sin_s[g * HALF_RD:(g + 1) * HALF_RD, :]

        def rot(a, width):
            a, b = a[:HALF_RD], a[HALF_RD:RD]
            c, s = cos[:, :width], sin[:, :width]
            return jnp.concatenate([a * c - b * s, b * c + a * s], 0)

        def unrot(a, width):
            a, b = a[:HALF_RD], a[HALF_RD:RD]
            c, s = cos[:, :width], sin[:, :width]
            return jnp.concatenate([a * c + b * s, b * c - a * s], 0)

        kr = rot(rope_s[g * RD:(g + 1) * RD, :], SEQ)
        kr_pad = jnp.concatenate([kr, jnp.zeros((HD - RD, SEQ), f32)], 0)
        k = kv[:, g * HD:(g + 1) * HD] + kr_pad.T
        k_s[...] = k.astype(bf16)
        kt_s[...] = k.T.astype(bf16)
        v_s[...] = kv[:, (GRP + g) * HD:(GRP + g + 1) * HD].astype(bf16)
        for c in range(NY):
            cols = slice(c * TOK, (c + 1) * TOK)
            qt_s[:, cols] = msg_ref[c, Q0 + g * TOK:Q0 + (g + 1) * TOK, :].astype(f32).T
            gt_s[:, cols] = msg_ref[c, G0 + g * TOK:G0 + (g + 1) * TOK, :].astype(f32).T.astype(bf16)
        qt_s[0:RD, :] = rot(qt_s[0:RD, :], HALF)
        qt = qt_s[...]
        q_s[...] = qt.T.astype(bf16)

        for b in range(HALF // BLK):
            cols = slice(b * BLK, (b + 1) * BLK)
            st = dot(k_s[...], qt[:, cols].astype(bf16))
            visible = pos_col <= pos_row[:, cols]
            st = jnp.where(visible, st * (scale * log2_e), neg_large)
            top = jnp.max(st, 0, keepdims=True)
            e = jnp.exp2(st - top)
            dp = dot(v_s[...], gt_s[:, cols])
            total = jnp.sum(e, 0, keepdims=True)
            weighted = jnp.sum(e * dp, 0, keepdims=True)
            inv_total = 1.0 / total
            delta = weighted * inv_total
            probs = (e * inv_total).astype(bf16)
            ds = (scale * probs.astype(f32) * (dp - delta)).astype(bf16)
            dqt_s[:, cols] = dot(kt_s[...], ds)
            dkv_s[:, g * HD:(g + 1) * HD] += dot(ds, q_s[cols, :])
            grad = jnp.concatenate(
                [
                    msg_ref[c, G0 + g * TOK:G0 + (g + 1) * TOK, :]
                    for c in range(b * BLK // TOK, (b + 1) * BLK // TOK)
                ],
                0,
            )
            dkv_s[:, (GRP + g) * HD:(GRP + g + 1) * HD] += dot(probs, grad)

        dqt_s[0:RD, :] = unrot(dqt_s[0:RD, :], HALF)
        dq = dqt_s[...].T.astype(bf16)
        dkr = unrot(dkv_s[:, g * HD:(g + 1) * HD].T[0:RD, :], SEQ).astype(bf16)
        for c in range(NY):
            cols = slice(c * TOK, (c + 1) * TOK)
            dq_ref[c, g * TOK:(g + 1) * TOK, :] = dq[cols, :]
            kr_own_ref[c, g * RD:(g + 1) * RD, :] = dkr[:, cols]
            kr_other_ref[c, g * RD:(g + 1) * RD, :] = dkr[:, HALF + c * TOK:HALF + (c + 1) * TOK]

    dkv = dkv_s[...].astype(bf16)
    dlat = dot(dkv, w_s[...], ((1,), (1,))).astype(bf16)
    for z in range(2):
        for y in range(NY):
            c = z * NY + y
            for b in range(TEN):
                lat_out_ref[y * TEN + b, z * TOK:(z + 1) * TOK, :] = dlat[
                    c * TOK:(c + 1) * TOK, b * HD:(b + 1) * HD
                ]
    dw_s[...] = dot(lat_s[...], dkv, ((0,), (0,)))
    for z in range(NZ):
        base = (z // 2) * CORE * 32 + (z % 2) * 16
        own = pl.ds(pl.multiple_of(base + core * 32, 16), 16)
        other = pl.ds(pl.multiple_of(base + (1 - core) * 32, 16), 16)
        dw_own_ref[z] = dw_s[own, :].astype(bf16)
        dw_other_ref[z] = dw_s[other, :].astype(bf16)


def attention(place, freq, msg, keys, w):
    smem = pl.BlockSpec(memory_space=pltpu.SMEM)
    vmem = pl.BlockSpec(memory_space=pltpu.VMEM)
    return pl.pallas_call(
        main_kernel,
        in_specs=[smem] + [vmem] * 7,
        out_specs=[vmem] * 6,
        out_shape=[
            jax.ShapeDtypeStruct((NY * TEN, 2 * TOK, HD), bf16),
            jax.ShapeDtypeStruct((NY, GRP * TOK, HD), bf16),
            jax.ShapeDtypeStruct((NY, GRP * RD, TOK), bf16),
            jax.ShapeDtypeStruct((NY, GRP * RD, TOK), bf16),
            jax.ShapeDtypeStruct((NZ, NY * ROWS, 2 * GRP * HD), bf16),
            jax.ShapeDtypeStruct((NZ, NY * ROWS, 2 * GRP * HD), bf16),
        ],
        scratch_shapes=[
            pltpu.VMEM((SEQ, RANK), bf16),
            pltpu.VMEM((RANK, 2 * GRP * HD), bf16),
            pltpu.VMEM((SEQ, HD), bf16),
            pltpu.VMEM((HD, SEQ), bf16),
            pltpu.VMEM((HALF, HD), bf16),
            pltpu.VMEM((HD, HALF), f32),
            pltpu.VMEM((SEQ, HD), bf16),
            pltpu.VMEM((HD, HALF), bf16),
            pltpu.VMEM((8, SEQ), f32),
            pltpu.VMEM((GRP * RD, SEQ), f32),
            pltpu.VMEM((GRP * HALF_RD, SEQ), f32),
            pltpu.VMEM((GRP * HALF_RD, SEQ), f32),
            pltpu.VMEM((SEQ, 2 * GRP * HD), f32),
            pltpu.VMEM((HD, HALF), f32),
            pltpu.VMEM((RANK, 2 * GRP * HD), f32),
        ],
        compiler_params=pltpu.CompilerParams(vmem_limit_bytes=56 * 1024 * 1024),
        name="attention_backward",
    )(place, freq, msg, *keys, w)


def fold_kernel(parts_ref, dw_ref, own_ref, other_ref, passed_ref):
    both = jnp.sum(parts_ref[...].astype(f32), 0)
    own_ref[...] = both[0:TOK]
    other_ref[...] = both[TOK:].astype(bf16)


def fold(parts, dw):
    vmem = pl.BlockSpec(memory_space=pltpu.VMEM)
    whole = pl.BlockSpec(memory_space=pl.ANY)
    return pl.pallas_call(
        fold_kernel,
        in_specs=[vmem, whole],
        out_specs=[vmem, vmem, whole],
        out_shape=[
            jax.ShapeDtypeStruct((TOK, HD), f32),
            jax.ShapeDtypeStruct((TOK, HD), bf16),
            jax.ShapeDtypeStruct(dw.shape, bf16),
        ],
        input_output_aliases={1: 2},
        name="fold",
    )(parts, dw)


def merge_kernel(own_ref, other_ref, kr0_ref, kr1_ref, quarter_ref, kr_ref):
    quarter_ref[...] = (own_ref[...] + other_ref[...].astype(f32)).astype(bf16)
    kr_ref[...] = (kr0_ref[...].astype(f32) + kr1_ref[...].astype(f32)).astype(bf16)


def merge(*parts):
    return pl.pallas_call(
        merge_kernel,
        out_shape=[
            jax.ShapeDtypeStruct((TOK, HD), bf16),
            jax.ShapeDtypeStruct((NY, GRP * RD, TOK), bf16),
        ],
        cost_estimate=waits_for_z,
        name="merge",
    )(*parts)


def combine_kernel(
    where_ref, dq_ref, kr_ref, dw_ref, q0_ref, q1_ref, pair_ref, out_ref, lat_ref
):
    x = where_ref[1]
    for t, ref in enumerate((q0_ref, q1_ref)):
        lat_ref[:, pl.ds(pl.multiple_of((x ^ t) * HD, HD), HD)] = ref[...]
    for t in range(2):
        cols = pl.ds(pl.multiple_of((x ^ 3 ^ t) * HD, HD), HD)
        lat_ref[:, cols] = pair_ref[t * TOK:(t + 1) * TOK, :]
    dw = jnp.sum(dw_ref[...].astype(f32), 0)
    for y in range(NY):
        out_ref[y, 0:BK0, :] = dq_ref[y]
        out_ref[y, BK0:BW0, :] = kr_ref[y]
        part = dw[y * ROWS:(y + 1) * ROWS, :]
        out_ref[y, BW0:BACK, :] = jnp.concatenate(
            [part[:, c * HD:(c + 1) * HD] for c in range(2 * GRP)], 0
        ).astype(bf16)


def combine(place, *parts):
    vmem = pl.BlockSpec(memory_space=pltpu.VMEM)
    return pl.pallas_call(
        combine_kernel,
        in_specs=[pl.BlockSpec(memory_space=pltpu.SMEM)] + [vmem] * 6,
        out_shape=[
            jax.ShapeDtypeStruct((NY, BACK, HD), bf16),
            jax.ShapeDtypeStruct((TOK, RANK), bf16),
        ],
        name="combine",
    )(place, *parts)


def unpack_kernel(msg_ref, q_ref, kr_ref, wk_ref, wv_ref):
    ropes = []
    wk = []
    wv = []
    for y in range(NY):
        for g in range(GRP):
            h = y * GRP + g
            q_ref[:, h * HD:(h + 1) * HD] = msg_ref[y, g * TOK:(g + 1) * TOK, :]
        ropes.append(msg_ref[y, BK0:BW0, :].astype(f32))
        tail = msg_ref[y, BW0:BACK, :].astype(f32)
        for g in range(GRP):
            wk.append(tail[g * ROWS:(g + 1) * ROWS, RD:])
            wv.append(tail[(GRP + g) * ROWS:(GRP + g + 1) * ROWS])
    kr_ref[...] = jnp.concatenate(ropes, 0).T.astype(bf16)
    wk_ref[...] = jnp.concatenate(wk, 1).astype(bf16)
    wv_ref[...] = jnp.concatenate(wv, 1).astype(bf16)


def unpack(msg):
    return pl.pallas_call(
        unpack_kernel,
        out_shape=[
            jax.ShapeDtypeStruct((TOK, NY * GRP * HD), bf16),
            jax.ShapeDtypeStruct((TOK, NY * GRP * RD), bf16),
            jax.ShapeDtypeStruct((ROWS, NY * GRP * NOPE), bf16),
            jax.ShapeDtypeStruct((ROWS, NY * GRP * HD), bf16),
        ],
        name="unpack",
    )(msg)


def swap(array, axis, size, flip):
    return lax.ppermute(array, axis, [(i, i ^ flip) for i in range(size)])


def body(latent, key_rope, query, out_grad, positions, freq_index, up_key, up_value):
    place = jnp.stack([lax.axis_index(a).astype(jnp.int32) for a in ("core", "x", "y", "zh")])

    msg, own = pack(query[0], out_grad[0], key_rope[0], latent[0], up_key, up_value, positions)
    other = swap(own, "zh", 2, 1)
    msg = lax.all_to_all(msg, "y", 0, 0)
    w = msg[:, W0:MSG, :].reshape(NY, 2 * GRP, ROWS, HD).transpose(1, 0, 2, 3)
    w = w.reshape(1, 2 * GRP * NY * ROWS, HD)
    w = lax.all_to_all(jnp.broadcast_to(w, (NZ,) + w.shape[1:]), ("zl", "zh"), 0, 0)
    keys = relay(place, other)
    keys = [keys[0]] + [swap(keys[t], "y", NY, t) for t in range(1, NY)]
    w = lax.all_gather(w, "core", axis=0)

    parts, dq, kr_own, kr_other, dw_own, dw_other = attention(place, freq_index, msg, keys, w)

    dw = (dw_own.astype(f32) + swap(dw_other, "core", 2, 1).astype(f32)).astype(bf16)
    parts = lax.all_to_all(parts, ("y", "x"), 0, 0)
    lat_own, other, dw = fold(parts, dw)
    other = swap(other, "zh", 2, 1)
    kr_other = swap(kr_other, "zh", 2, 1)
    dw = lax.all_to_all(dw, ("zl", "zh"), 0, 0)
    quarter, kr = merge(lat_own, other, kr_own, kr_other)
    next_quarter = swap(quarter, "x", TEN, 1)
    pair = swap(jnp.concatenate([quarter, next_quarter], 0), "x", TEN, 3)
    back, latent_grad = combine(place, dq, kr, dw, quarter, next_quarter, pair)
    back = lax.all_to_all(back, "y", 0, 0)
    query_grad, key_rope_grad, up_key_grad, up_value_grad = unpack(back)
    return (query_grad[None], key_rope_grad[None], latent_grad[None], up_key_grad, up_value_grad)


def solution(mesh):
    split = Mesh(mesh.devices.reshape(ZL, CORE, 2, NY, TEN), ("zl", "core", "zh", "y", "x"))
    dp, context, tensor = ("zl", "core"), ("zh", "y"), "x"
    return jax.shard_map(
        body,
        mesh=split,
        in_specs=(
            P(dp, context, None),
            P(dp, context, tensor),
            P(dp, context, tensor),
            P(dp, context, tensor),
            P(dp, context),
            P(tensor, None),
            P(dp + context, tensor),
            P(dp + context, tensor),
        ),
        out_specs=(
            P(dp, context, tensor),
            P(dp, context, tensor),
            P(dp, context, None),
            P(dp + context, tensor),
            P(dp + context, tensor),
        ),
        check_vma=False,
    )
```

```python
import math

import jax
import jax.numpy as jnp
from jax import lax
from jax.experimental import pallas as pl
from jax.experimental.pallas import tpu as pltpu
from jax.sharding import Mesh, PartitionSpec as P

rope_base = 500000.0
neg_large = -1e30
log2_e = 1.4426950408889634

NY = 4
GRP = 2
TOK = 128
HALF = NY * TOK
SEQ = 2 * HALF
HD = 128
RD = 32
HALF_RD = 16
NOPE = 96
RANK = 512
ROWS = 4
ZL = 8
CORE = 2
NZ = 2 * ZL
TEN = 4
Q0, G0, L0, K0, S0, W0, MSG = 0, 256, 512, 1024, 1088, 1104, 1120
KEY_K, KEY_S, KEY = 512, 768, 784
PASS_S, PASS = 576, 592
BK0, BW0, BACK = 256, 320, 336
BLK = 512

waits_for_z = pl.CostEstimate(flops=50_000_000_000, transcendentals=0, bytes_accessed=150_000_000)
f32 = jnp.float32
bf16 = jnp.bfloat16


def dot(a, b, dims=((1,), (0,))):
    return lax.dot_general(a, b, (dims, ((), ())), preferred_element_type=f32)


def pack_kernel(q_ref, g_ref, kr_ref, lat_ref, wk_ref, wv_ref, pos_ref, out_ref, key_ref):
    rope_t = kr_ref[...].astype(f32).T.astype(bf16)
    pos = pos_ref[...]
    places = jnp.concatenate(
        [(pos >> 6).astype(f32), (pos & 63).astype(f32), jnp.zeros((14, TOK), f32)], 0
    ).astype(bf16)
    for b in range(RANK // HD):
        key_ref[b * TOK:(b + 1) * TOK, :] = lat_ref[:, b * HD:(b + 1) * HD]
    key_ref[KEY_K:KEY_S, :] = rope_t
    key_ref[KEY_S:KEY, :] = places
    wk = wk_ref[...].astype(f32)
    wv = wv_ref[...].astype(f32)
    for y in range(NY):
        parts_k = []
        parts_v = []
        for g in range(GRP):
            h = y * GRP + g
            cols = slice(h * HD, (h + 1) * HD)
            out_ref[y, Q0 + g * TOK:Q0 + (g + 1) * TOK, :] = q_ref[:, cols]
            out_ref[y, G0 + g * TOK:G0 + (g + 1) * TOK, :] = g_ref[:, cols]
            parts_v.append(wv[:, cols])
            parts_k.append(
                jnp.concatenate([jnp.zeros((ROWS, RD), f32), wk[:, h * NOPE:(h + 1) * NOPE]], 1)
            )
        for b in range(RANK // HD):
            out_ref[y, L0 + b * TOK:L0 + (b + 1) * TOK, :] = lat_ref[:, b * HD:(b + 1) * HD]
        out_ref[y, K0:S0, :] = rope_t[y * GRP * RD:(y + 1) * GRP * RD, :]
        out_ref[y, S0:W0, :] = places
        out_ref[y, W0:MSG, :] = jnp.concatenate(parts_k + parts_v, 0).astype(bf16)


def pack(*parts):
    return pl.pallas_call(
        pack_kernel,
        out_shape=[
            jax.ShapeDtypeStruct((NY, MSG, HD), bf16),
            jax.ShapeDtypeStruct((KEY, HD), bf16),
        ],
        name="pack",
    )(*parts)


def relay_kernel(where_ref, key_ref, *out_refs):
    own_y = where_ref[2]
    for t, ref in enumerate(out_refs):
        rows = KEY_K + (own_y ^ t) * (GRP * RD)
        ref[0:KEY_K, :] = key_ref[0:KEY_K, :]
        ref[KEY_K:PASS_S, :] = key_ref[pl.ds(pl.multiple_of(rows, GRP * RD), GRP * RD), :]
        ref[PASS_S:PASS, :] = key_ref[KEY_S:KEY, :]


def relay(place, other):
    return pl.pallas_call(
        relay_kernel,
        in_specs=[
            pl.BlockSpec(memory_space=pltpu.SMEM),
            pl.BlockSpec(memory_space=pltpu.VMEM),
        ],
        out_shape=[jax.ShapeDtypeStruct((PASS, HD), bf16)] * NY,
        cost_estimate=waits_for_z,
        name="relay",
    )(place, other)


def main_kernel(
    where_ref, freq_ref, msg_ref, key0_ref, key1_ref, key2_ref, key3_ref, w_ref,
    lat_out_ref, dq_ref, kr_own_ref, kr_other_ref, dw_own_ref, dw_other_ref,
    lat_s, w_s, k_s, kt_s, q_s, qt_s, v_s, gt_s, pos_s, rope_s, cos_s, sin_s, dkv_s, dqt_s, dw_s,
):
    core = where_ref[0]
    own_y = where_ref[2]
    def take(read, lat0, rope0, pos0, tokens):
        for b in range(RANK // HD):
            lat_s[tokens, b * HD:(b + 1) * HD] = read(lat0 + b * TOK, TOK)
        rope_s[:, tokens] = read(rope0, GRP * RD).astype(f32)
        tail = read(pos0, 16).astype(f32)
        pos_s[0:1, tokens] = tail[0:1] * 64.0 + tail[1:2]

    for y in range(NY):
        take(
            lambda r, n, y=y: msg_ref[y, r:r + n, :], L0, K0, S0,
            slice(y * TOK, (y + 1) * TOK),
        )
    for t, ref in enumerate((key0_ref, key1_ref, key2_ref, key3_ref)):
        tokens = pl.ds(pl.multiple_of((NY + (own_y ^ t)) * TOK, TOK), TOK)
        take(lambda r, n, ref=ref: ref[r:r + n, :], 0, KEY_K, PASS_S, tokens)
    for z in range(NZ):
        for c in range(CORE):
            r = ((z // 2) * CORE + c) * 32 + (z % 2) * 16
            for kind in range(2 * GRP):
                w_s[r:r + 16, kind * HD:(kind + 1) * HD] = w_ref[c, z, kind * 16:(kind + 1) * 16, :]
    pos_row = pos_s[0:1, :]
    freq = freq_ref[...].astype(f32)
    heads = lax.broadcasted_iota(jnp.int32, freq.shape, 0)
    diagonal = lax.broadcasted_iota(jnp.int32, (HALF_RD, HALF_RD), 0) == lax.broadcasted_iota(
        jnp.int32, (HALF_RD, HALF_RD), 1
    )
    columns = []
    for g in range(GRP):
        row = jnp.sum(jnp.where(heads == own_y * GRP + g, freq, 0.0), 0, keepdims=True)
        columns.append(jnp.sum(jnp.where(diagonal, row, 0.0), 1, keepdims=True))
    inverse = jnp.exp(jnp.concatenate(columns, 0) * (-2.0 / HD * math.log(rope_base)))
    angles = inverse * pos_row
    cos_s[...] = jnp.cos(angles)
    sin_s[...] = jnp.sin(angles)
    pos_col = jnp.broadcast_to(pos_row, (8, SEQ)).T[:, 0:1]
    scale = HD ** -0.5
    kv = dot(lat_s[...], w_s[...])
    dkv_s[...] = jnp.zeros_like(dkv_s)

    for g in range(GRP):
        cos = cos_s[g * HALF_RD:(g + 1) * HALF_RD, :]
        sin = sin_s[g * HALF_RD:(g + 1) * HALF_RD, :]

        def rot(a, width):
            a, b = a[:HALF_RD], a[HALF_RD:RD]
            c, s = cos[:, :width], sin[:, :width]
            return jnp.concatenate([a * c - b * s, b * c + a * s], 0)

        def unrot(a, width):
            a, b = a[:HALF_RD], a[HALF_RD:RD]
            c, s = cos[:, :width], sin[:, :width]
            return jnp.concatenate([a * c + b * s, b * c - a * s], 0)

        kr = rot(rope_s[g * RD:(g + 1) * RD, :], SEQ)
        kr_pad = jnp.concatenate([kr, jnp.zeros((HD - RD, SEQ), f32)], 0)
        k = kv[:, g * HD:(g + 1) * HD] + kr_pad.T
        k_s[...] = k.astype(bf16)
        kt_s[...] = k.T.astype(bf16)
        v_s[...] = kv[:, (GRP + g) * HD:(GRP + g + 1) * HD].astype(bf16)
        for c in range(NY):
            cols = slice(c * TOK, (c + 1) * TOK)
            qt_s[:, cols] = msg_ref[c, Q0 + g * TOK:Q0 + (g + 1) * TOK, :].astype(f32).T
            gt_s[:, cols] = msg_ref[c, G0 + g * TOK:G0 + (g + 1) * TOK, :].astype(f32).T.astype(bf16)
        qt_s[0:RD, :] = rot(qt_s[0:RD, :], HALF)
        qt = qt_s[...]
        q_s[...] = qt.T.astype(bf16)

        for b in range(HALF // BLK):
            cols = slice(b * BLK, (b + 1) * BLK)
            st = dot(k_s[...], qt[:, cols].astype(bf16))
            visible = pos_col <= pos_row[:, cols]
            st = jnp.where(visible, st * (scale * log2_e), neg_large)
            top = jnp.max(st, 0, keepdims=True)
            e = jnp.exp2(st - top)
            dp = dot(v_s[...], gt_s[:, cols])
            total = jnp.sum(e, 0, keepdims=True)
            weighted = jnp.sum(e * dp, 0, keepdims=True)
            inv_total = 1.0 / total
            delta = weighted * inv_total
            probs = (e * inv_total).astype(bf16)
            ds = (scale * probs.astype(f32) * (dp - delta)).astype(bf16)
            dqt_s[:, cols] = dot(kt_s[...], ds)
            dkv_s[:, g * HD:(g + 1) * HD] += dot(ds, q_s[cols, :])
            grad = jnp.concatenate(
                [
                    msg_ref[c, G0 + g * TOK:G0 + (g + 1) * TOK, :]
                    for c in range(b * BLK // TOK, (b + 1) * BLK // TOK)
                ],
                0,
            )
            dkv_s[:, (GRP + g) * HD:(GRP + g + 1) * HD] += dot(probs, grad)

        dqt_s[0:RD, :] = unrot(dqt_s[0:RD, :], HALF)
        dq = dqt_s[...].T.astype(bf16)
        dkr = unrot(dkv_s[:, g * HD:(g + 1) * HD].T[0:RD, :], SEQ).astype(bf16)
        for c in range(NY):
            cols = slice(c * TOK, (c + 1) * TOK)
            dq_ref[c, g * TOK:(g + 1) * TOK, :] = dq[cols, :]
            kr_own_ref[c, g * RD:(g + 1) * RD, :] = dkr[:, cols]
            kr_other_ref[c, g * RD:(g + 1) * RD, :] = dkr[:, HALF + c * TOK:HALF + (c + 1) * TOK]

    dkv = dkv_s[...].astype(bf16)
    dlat = dot(dkv, w_s[...], ((1,), (1,))).astype(bf16)
    for z in range(2):
        for y in range(NY):
            c = z * NY + y
            for b in range(TEN):
                lat_out_ref[y * TEN + b, z * TOK:(z + 1) * TOK, :] = dlat[
                    c * TOK:(c + 1) * TOK, b * HD:(b + 1) * HD
                ]
    dw_s[...] = dot(lat_s[...], dkv, ((0,), (0,)))
    for z in range(NZ):
        base = (z % ZL) * CORE * 32 + (z // ZL) * 16
        own = pl.ds(pl.multiple_of(base + core * 32, 16), 16)
        other = pl.ds(pl.multiple_of(base + (1 - core) * 32, 16), 16)
        dw_own_ref[z] = dw_s[own, :].astype(bf16)
        dw_other_ref[z] = dw_s[other, :].astype(bf16)


def attention(place, freq, msg, keys, w):
    smem = pl.BlockSpec(memory_space=pltpu.SMEM)
    vmem = pl.BlockSpec(memory_space=pltpu.VMEM)
    return pl.pallas_call(
        main_kernel,
        in_specs=[smem] + [vmem] * 7,
        out_specs=[vmem] * 6,
        out_shape=[
            jax.ShapeDtypeStruct((NY * TEN, 2 * TOK, HD), bf16),
            jax.ShapeDtypeStruct((NY, GRP * TOK, HD), bf16),
            jax.ShapeDtypeStruct((NY, GRP * RD, TOK), bf16),
            jax.ShapeDtypeStruct((NY, GRP * RD, TOK), bf16),
            jax.ShapeDtypeStruct((NZ, NY * ROWS, 2 * GRP * HD), bf16),
            jax.ShapeDtypeStruct((NZ, NY * ROWS, 2 * GRP * HD), bf16),
        ],
        scratch_shapes=[
            pltpu.VMEM((SEQ, RANK), bf16),
            pltpu.VMEM((RANK, 2 * GRP * HD), bf16),
            pltpu.VMEM((SEQ, HD), bf16),
            pltpu.VMEM((HD, SEQ), bf16),
            pltpu.VMEM((HALF, HD), bf16),
            pltpu.VMEM((HD, HALF), f32),
            pltpu.VMEM((SEQ, HD), bf16),
            pltpu.VMEM((HD, HALF), bf16),
            pltpu.VMEM((8, SEQ), f32),
            pltpu.VMEM((GRP * RD, SEQ), f32),
            pltpu.VMEM((GRP * HALF_RD, SEQ), f32),
            pltpu.VMEM((GRP * HALF_RD, SEQ), f32),
            pltpu.VMEM((SEQ, 2 * GRP * HD), f32),
            pltpu.VMEM((HD, HALF), f32),
            pltpu.VMEM((RANK, 2 * GRP * HD), f32),
        ],
        compiler_params=pltpu.CompilerParams(vmem_limit_bytes=56 * 1024 * 1024),
        name="attention_backward",
    )(place, freq, msg, *keys, w)


def fold_kernel(parts_ref, dw_ref, own_ref, other_ref, passed_ref):
    both = jnp.sum(parts_ref[...].astype(f32), 0)
    own_ref[...] = both[0:TOK]
    other_ref[...] = both[TOK:].astype(bf16)


def fold(parts, dw):
    vmem = pl.BlockSpec(memory_space=pltpu.VMEM)
    whole = pl.BlockSpec(memory_space=pl.ANY)
    return pl.pallas_call(
        fold_kernel,
        in_specs=[vmem, whole],
        out_specs=[vmem, vmem, whole],
        out_shape=[
            jax.ShapeDtypeStruct((TOK, HD), f32),
            jax.ShapeDtypeStruct((TOK, HD), bf16),
            jax.ShapeDtypeStruct(dw.shape, bf16),
        ],
        input_output_aliases={1: 2},
        name="fold",
    )(parts, dw)


def merge_kernel(own_ref, other_ref, kr0_ref, kr1_ref, quarter_ref, kr_ref):
    quarter_ref[...] = (own_ref[...] + other_ref[...].astype(f32)).astype(bf16)
    kr_ref[...] = (kr0_ref[...].astype(f32) + kr1_ref[...].astype(f32)).astype(bf16)


def merge(*parts):
    return pl.pallas_call(
        merge_kernel,
        out_shape=[
            jax.ShapeDtypeStruct((TOK, HD), bf16),
            jax.ShapeDtypeStruct((NY, GRP * RD, TOK), bf16),
        ],
        cost_estimate=waits_for_z,
        name="merge",
    )(*parts)


def combine_kernel(
    where_ref, dq_ref, kr_ref, dw_ref, q0_ref, q1_ref, pair_ref, out_ref, lat_ref
):
    x = where_ref[1]
    for t, ref in enumerate((q0_ref, q1_ref)):
        lat_ref[:, pl.ds(pl.multiple_of((x ^ t) * HD, HD), HD)] = ref[...]
    for t in range(2):
        cols = pl.ds(pl.multiple_of((x ^ 3 ^ t) * HD, HD), HD)
        lat_ref[:, cols] = pair_ref[t * TOK:(t + 1) * TOK, :]
    dw = jnp.sum(dw_ref[...].astype(f32), 0)
    for y in range(NY):
        out_ref[y, 0:BK0, :] = dq_ref[y]
        out_ref[y, BK0:BW0, :] = kr_ref[y]
        part = dw[y * ROWS:(y + 1) * ROWS, :]
        out_ref[y, BW0:BACK, :] = jnp.concatenate(
            [part[:, c * HD:(c + 1) * HD] for c in range(2 * GRP)], 0
        ).astype(bf16)


def combine(place, *parts):
    vmem = pl.BlockSpec(memory_space=pltpu.VMEM)
    return pl.pallas_call(
        combine_kernel,
        in_specs=[pl.BlockSpec(memory_space=pltpu.SMEM)] + [vmem] * 6,
        out_shape=[
            jax.ShapeDtypeStruct((NY, BACK, HD), bf16),
            jax.ShapeDtypeStruct((TOK, RANK), bf16),
        ],
        name="combine",
    )(place, *parts)


def unpack_kernel(msg_ref, q_ref, kr_ref, wk_ref, wv_ref):
    ropes = []
    wk = []
    wv = []
    for y in range(NY):
        for g in range(GRP):
            h = y * GRP + g
            q_ref[:, h * HD:(h + 1) * HD] = msg_ref[y, g * TOK:(g + 1) * TOK, :]
        ropes.append(msg_ref[y, BK0:BW0, :].astype(f32))
        tail = msg_ref[y, BW0:BACK, :].astype(f32)
        for g in range(GRP):
            wk.append(tail[g * ROWS:(g + 1) * ROWS, RD:])
            wv.append(tail[(GRP + g) * ROWS:(GRP + g + 1) * ROWS])
    kr_ref[...] = jnp.concatenate(ropes, 0).T.astype(bf16)
    wk_ref[...] = jnp.concatenate(wk, 1).astype(bf16)
    wv_ref[...] = jnp.concatenate(wv, 1).astype(bf16)


def unpack(msg):
    return pl.pallas_call(
        unpack_kernel,
        out_shape=[
            jax.ShapeDtypeStruct((TOK, NY * GRP * HD), bf16),
            jax.ShapeDtypeStruct((TOK, NY * GRP * RD), bf16),
            jax.ShapeDtypeStruct((ROWS, NY * GRP * NOPE), bf16),
            jax.ShapeDtypeStruct((ROWS, NY * GRP * HD), bf16),
        ],
        name="unpack",
    )(msg)


def swap(array, axis, size, flip):
    return lax.ppermute(array, axis, [(i, i ^ flip) for i in range(size)])


def body(latent, key_rope, query, out_grad, positions, freq_index, up_key, up_value):
    place = jnp.stack([lax.axis_index(a).astype(jnp.int32) for a in ("core", "x", "y", "zh")])

    msg, own = pack(query[0], out_grad[0], key_rope[0], latent[0], up_key, up_value, positions)
    other = swap(own, "zh", 2, 1)
    msg = lax.all_to_all(msg, "y", 0, 0)
    w = msg[:, W0:MSG, :].reshape(NY, 2 * GRP, ROWS, HD).transpose(1, 0, 2, 3)
    w = w.reshape(1, 2 * GRP * NY * ROWS, HD)
    w = lax.all_to_all(jnp.broadcast_to(w, (NZ,) + w.shape[1:]), ("zl", "zh"), 0, 0)
    keys = relay(place, other)
    keys = [keys[0]] + [swap(keys[t], "y", NY, t) for t in range(1, NY)]
    w = lax.all_gather(w, "core", axis=0)

    parts, dq, kr_own, kr_other, dw_own, dw_other = attention(place, freq_index, msg, keys, w)

    dw = (dw_own.astype(f32) + swap(dw_other, "core", 2, 1).astype(f32)).astype(bf16)
    parts = lax.all_to_all(parts, ("y", "x"), 0, 0)
    lat_own, other, dw = fold(parts, dw)
    other = swap(other, "zh", 2, 1)
    kr_other = swap(kr_other, "zh", 2, 1)
    dw = lax.all_to_all(dw, ("zh", "zl"), 0, 0)
    quarter, kr = merge(lat_own, other, kr_own, kr_other)
    next_quarter = swap(quarter, "x", TEN, 1)
    pair = swap(jnp.concatenate([quarter, next_quarter], 0), "x", TEN, 3)
    back, latent_grad = combine(place, dq, kr, dw, quarter, next_quarter, pair)
    back = lax.all_to_all(back, "y", 0, 0)
    query_grad, key_rope_grad, up_key_grad, up_value_grad = unpack(back)
    return (query_grad[None], key_rope_grad[None], latent_grad[None], up_key_grad, up_value_grad)


def solution(mesh):
    split = Mesh(mesh.devices.reshape(ZL, CORE, 2, NY, TEN), ("zl", "core", "zh", "y", "x"))
    dp, context, tensor = ("zl", "core"), ("zh", "y"), "x"
    return jax.shard_map(
        body,
        mesh=split,
        in_specs=(
            P(dp, context, None),
            P(dp, context, tensor),
            P(dp, context, tensor),
            P(dp, context, tensor),
            P(dp, context),
            P(tensor, None),
            P(dp + context, tensor),
            P(dp + context, tensor),
        ),
        out_specs=(
            P(dp, context, tensor),
            P(dp, context, tensor),
            P(dp, context, None),
            P(dp + context, tensor),
            P(dp + context, tensor),
        ),
        check_vma=False,
    )
```
